1024 devices in a mesh: mem: 64 (over y, x_hi, core), dom: 16 (over z, x_lo).
Axes of the slice: x: 8 (x_hi: 4, x_lo: 2; x = x_hi * 2 + x_lo), y: 8, z: 8, core: 2. Of those that a mesh axis runs over, the one named last changes fastest.
Arguments:
- prior_sample: bfloat16 [512, 8, 256, 256], P('mem', None, 'dom'), may hold values from -4 to 4
- prior_velocity: float32 [2, 8, 256], replicated, may hold values from -0.8 to 0.8
- obs_cells: int32 [16, 64, 128], P('dom', 'mem'), may hold values from 0 to 511
- obs_bins: int32 [16, 64, 128], P('dom', 'mem'), may hold values from 0 to 7
- obs_values: float32 [16, 64, 128], P('dom', 'mem'), may hold values from -6 to 6
- tile_owner: int32 [16, 64], P('dom'), may hold values from 0 to 63, each once within a row
Outputs:
- analysis: bfloat16 [512, 8, 256, 256], P('mem', None, 'dom')
The draws below stay inside these ranges and needn't reach their ends.
Inputs may be any that keep to these rules, and one draw needn't show every extreme that they name: `obs_cells`: index 256 * (row within the tile) + column. `tile_owner`: each row names every slot once.
All inputs are finite; a program needn't handle non-finite values. Where the reference program divides by a largest or mean magnitude, that divisor is 1e-20 or more.
Results may differ from the reference program's by a relative error of at most 0.0082.
Values may be sent and summed in bfloat16 or wider, within the bound.
No kernel may reach another device: no remote copies, remote signals or barrier semaphores. Data moves between devices by JAX's collectives and lax.ppermute only.
A program may use at most 32 MiB of HBM per device.

```python
import jax
import jax.numpy as jnp
from jax import lax

MEMBER_TOTAL = 512
LATTICE_WIDTH = 256
LAYER_TOTAL = 8
TPD = 1
OBS = 128
NBINS = 8
STEPS = 5
TILE = 512
PATCH_HEIGHT = 16
NY = 256
N_MEM = 64
N_DOM = 16


def draw_prior_sample(key, part):
    keys = jax.random.split(jax.random.fold_in(key, 71), 2)
    common = jax.random.normal(keys[0], (LAYER_TOTAL, NY, LATTICE_WIDTH), jnp.float32) * 0.7
    members = jax.random.normal(keys[1], (MEMBER_TOTAL, LAYER_TOTAL, NY, LATTICE_WIDTH), jnp.float32)
    field = common + members
    return jnp.clip(field, -4.0, 4.0).astype(jnp.bfloat16)


def with_ends(result, own_key, smallest, largest):
    extent = result.shape
    place = [jax.random.randint(jax.random.fold_in(own_key, axis), (), 0, extent[axis]) for axis in range(len(extent))]
    result = result.at[tuple(place)].set(smallest)
    longest = extent.index(max(extent))
    place[longest] = (place[longest] + 1) % extent[longest]
    return result.at[tuple(place)].set(largest)


def steps_of(key, shape, pieces, low, top_value):
    def one(position, shards_of):
        heights = jax.random.uniform(jax.random.fold_in(jax.random.fold_in(key, 6), position), (shards_of,), jnp.float32, low / len(pieces), top_value / len(pieces))
        return jnp.repeat(jnp.exp(heights), shape[position] // shards_of).reshape((-1,) + (1,) * (len(shape) - position - 1))

    level = one(*pieces[0])
    for cut in pieces[1:]:
        level = level * one(*cut)
    return level


def noise(stream_key, shape, scale, most, shards=(), held_as=jnp.bfloat16):
    array = scale * jax.random.normal(stream_key, shape, jnp.float32)
    if shards:
        array = array * steps_of(stream_key, shape, shards, -0.22, 0.18)
    return jnp.clip(array, -most, most).astype(held_as)


def setup_inputs(seed: int = 0) -> dict:
    arg_keys = jax.random.split(jax.random.key(seed), 7)
    prior_sample = draw_prior_sample(jax.random.fold_in(arg_keys[6], 71), 0)
    prior_velocity = jnp.clip(jax.random.uniform(arg_keys[1], (2, LAYER_TOTAL, LATTICE_WIDTH), jnp.float32, -0.8, 0.8), -0.8, 0.8)
    obs_cells = with_ends(jax.random.randint(arg_keys[2], (N_DOM, N_MEM * TPD, OBS), 0, TILE), jax.random.fold_in(arg_keys[2], 1), 0, TILE - 1).astype(jnp.int32)
    obs_bins = with_ends(jax.random.randint(arg_keys[3], (N_DOM, N_MEM * TPD, OBS), 0, NBINS), jax.random.fold_in(arg_keys[3], 1), 0, NBINS - 1).astype(jnp.int32)
    obs_values = noise(arg_keys[4], (N_DOM, N_MEM * TPD, OBS), 1.0, 6.0, ((0, 16), (1, 64)), jnp.float32)
    tile_owner = jax.vmap(lambda own: jax.random.permutation(own, N_MEM * TPD))(jax.random.split(arg_keys[5], N_DOM)).reshape((N_DOM, N_MEM * TPD)).astype(jnp.int32)
    return {"prior_sample": prior_sample, "prior_velocity": prior_velocity, "obs_cells": obs_cells, "obs_bins": obs_bins, "obs_values": obs_values, "tile_owner": tile_owner}


advect_coef = 0.15
diffuse_coef = 0.15
loc_step = 0.35
inflation = 1.1

def propagate_prior(haloed_field, prior_velocity):
    centre = haloed_field[..., 1:-1, :]
    along_x = prior_velocity[0][:, None, :]
    along_y = prior_velocity[1][:, None, :]
    flux_x = (along_x + 0.5 * centre) * centre
    flux_y = (along_y + 0.5 * haloed_field) * haloed_field
    east = jnp.roll(flux_x, -1, axis=-1)
    west = jnp.roll(flux_x, 1, axis=-1)
    neighbours = jnp.roll(centre, -1, axis=-1) + jnp.roll(centre, 1, axis=-1) + haloed_field[..., 2:, :] + haloed_field[..., :-2, :]
    return centre - advect_coef * (east - west + flux_y[..., 2:, :] - flux_y[..., :-2, :]) + diffuse_coef * (neighbours - 4.0 * centre)

def cyclic_field(field):
    return jnp.concatenate([field[:, -1:], field, field[:, :1]], axis=1)

def widened(left, right):
    return jnp.dot(left.astype(jnp.float32), right.astype(jnp.float32), precision=lax.Precision.HIGHEST)

def analyse(ensemble, obs_at, radius_bins, observed):
    members = ensemble.shape[0]
    values_wide = ensemble.astype(jnp.float32)
    average = lax.optimization_barrier(jnp.mean(values_wide, axis=0))
    spread = (values_wide - average).astype(jnp.bfloat16)
    picked = jnp.take(spread, obs_at, axis=1)
    innovation = observed - jnp.take(average, obs_at)
    weights = jnp.exp(-0.5 * (loc_step * radius_bins.astype(jnp.float32)) ** 2)
    scaled = (picked.astype(jnp.float32) * weights).astype(jnp.bfloat16)
    eye_wide = jnp.eye(members, dtype=jnp.float32)
    matrix = widened(picked, scaled.astype(jnp.float32).T)
    matrix = matrix + (members - 1) / inflation * eye_wide
    norm_total = jnp.max(lax.optimization_barrier(jnp.sum(jnp.abs(matrix), axis=1)))
    current_y = (matrix / norm_total).astype(jnp.bfloat16)
    factor = (1.5 * eye_wide - 0.5 * current_y.astype(jnp.float32)).astype(jnp.bfloat16)
    current_y = widened(current_y, factor).astype(jnp.bfloat16)
    current_z = factor
    for sweep_number in range(1, STEPS):
        product = widened(current_z, current_y)
        factor = (1.5 * eye_wide - 0.5 * product).astype(jnp.bfloat16)
        if sweep_number + 1 < STEPS:
            current_y = widened(current_y, factor).astype(jnp.bfloat16)
        current_z = widened(factor, current_z).astype(jnp.bfloat16)
    inverse_root = current_z.astype(jnp.float32)
    forcing = jnp.dot(picked.astype(jnp.float32), weights * innovation, precision=lax.Precision.HIGHEST)
    inner = jnp.dot(inverse_root, forcing, precision=lax.Precision.HIGHEST)
    shift = jnp.dot(inverse_root, inner, precision=lax.Precision.HIGHEST) / norm_total
    transform = (jnp.sqrt((members - 1) / norm_total) * inverse_root + shift[:, None]).astype(jnp.bfloat16)
    update = widened(transform.astype(jnp.float32).T, spread)
    return (average + update).astype(jnp.bfloat16)

def reference(prior_sample, prior_velocity, obs_cells, obs_bins, obs_values, tile_owner):

    def lone_realisation(realisation):
        leading = propagate_prior(cyclic_field(realisation.astype(jnp.float32)), prior_velocity)
        return propagate_prior(cyclic_field(leading), prior_velocity).astype(jnp.bfloat16)
    prior_field = lax.map(lone_realisation, prior_sample)
    slot_count = N_MEM * TPD
    window_pieces = prior_field.reshape(MEMBER_TOTAL, LAYER_TOTAL, N_DOM, PATCH_HEIGHT, LATTICE_WIDTH).transpose(2, 0, 1, 3, 4)
    window_pieces = window_pieces.reshape(N_DOM, MEMBER_TOTAL, slot_count, TILE).transpose(0, 2, 1, 3)
    window_pieces = window_pieces.reshape(N_DOM * slot_count, MEMBER_TOTAL, TILE)

    def pick_rows(table, owners):
        return jnp.take(table, owners, axis=0)
    obs_at = jax.vmap(pick_rows)(obs_cells, tile_owner).reshape(N_DOM * slot_count, OBS)
    radius_bins = jax.vmap(pick_rows)(obs_bins, tile_owner).reshape(N_DOM * slot_count, OBS)
    observed = jax.vmap(pick_rows)(obs_values, tile_owner).reshape(N_DOM * slot_count, OBS)
    updated = lax.map(lambda item: analyse(item[0], item[1], item[2], item[3]), (window_pieces, obs_at, radius_bins, observed))
    updated = updated.reshape(N_DOM, slot_count, MEMBER_TOTAL, TILE).transpose(2, 0, 1, 3)
    updated = updated.reshape(MEMBER_TOTAL, N_DOM, LAYER_TOTAL, PATCH_HEIGHT, LATTICE_WIDTH).transpose(0, 2, 1, 3, 4)
    return updated.reshape(MEMBER_TOTAL, LAYER_TOTAL, NY, LATTICE_WIDTH)
```

```python
import functools

import jax
import jax.numpy as jnp
from jax import lax
from jax.experimental import pallas as pl
from jax.experimental.pallas import tpu as pltpu
from jax.sharding import Mesh
from jax.sharding import PartitionSpec as P

STEPS = 5
MEM = ("mem_0", "mem_1", "mem_2")

advect_coef = 0.15
diffuse_coef = 0.15
loc_step = 0.35
inflation = 1.1

F32 = jnp.float32
BF16 = jnp.bfloat16
VMEM = pl.BlockSpec(memory_space=pltpu.VMEM)
SMEM = pl.BlockSpec(memory_space=pltpu.SMEM)
PARAMS = pltpu.CompilerParams(vmem_limit_bytes=48 * 1024 * 1024)


def rows_first(block):
    return jnp.swapaxes(block.astype(F32), 0, 1)


def step(rows, along_x, along_y):
    width = rows[0].shape[-1]
    below, above, inner = [], [], []
    last = len(rows) - 1
    for r, v in enumerate(rows):
        half = 0.5 * v
        flux_y = (along_y + half) * v
        below.append(v - flux_y if r >= 2 else None)
        above.append(v + flux_y if r <= last - 2 else None)
        if 1 <= r <= last - 1:
            flux_x = (along_x + half) * v
            east = pltpu.roll(v - flux_x, width - 1, axis=1)
            west = pltpu.roll(v + flux_x, 1, axis=1)
            inner.append((east + west) - 4.0 * v)
        else:
            inner.append(None)
    return [
        rows[r] + advect_coef * (inner[r] + (below[r + 1] + above[r - 1]))
        for r in range(1, last)
    ]


def edges_kernel(x_ref, low_ref, high_ref):
    levels, rows = x_ref.shape[1], x_ref.shape[2]
    for level in range(levels):
        block = x_ref[:, level]
        low_ref[level] = rows_first(block[:, 0:2]).astype(BF16)
        high_ref[level] = rows_first(block[:, rows - 2 : rows]).astype(BF16)


def put(out_ref, slot, rows, width):
    out_ref[slot, :, 0:width] = rows[0].astype(BF16)
    out_ref[slot, :, width : 2 * width] = rows[1].astype(BF16)


def interior_kernel(owner_ref, velocity_ref, x_ref, out_ref):
    members, levels, rows, width = x_ref.shape
    pairs = rows // 2

    def one(level, carry):
        along_x = velocity_ref[0, pl.ds(level, 1), :]
        along_y = velocity_ref[1, pl.ds(level, 1), :]
        field = rows_first(x_ref[:, level])
        done = [field[r] for r in range(rows)]
        for _ in range(2):
            done = step(done, along_x, along_y)
        for p in range(1, pairs - 1):
            put(out_ref, owner_ref[0, level * pairs + p], done[2 * p - 2 : 2 * p], width)
        return carry

    lax.fori_loop(0, levels, one, 0)


def outer_kernel(owner_ref, velocity_ref, x_ref, before_ref, after_ref, partial_ref, out_ref):
    members, levels, rows, width = x_ref.shape
    pairs = rows // 2
    out_ref[...] = partial_ref[...]

    def one(level, carry):
        along_x = velocity_ref[0, pl.ds(level, 1), :]
        along_y = velocity_ref[1, pl.ds(level, 1), :]
        field = rows_first(x_ref[:, level])
        before = before_ref[level].astype(F32)
        after = after_ref[level].astype(F32)
        top = [before[0], before[1]] + [field[r] for r in range(4)]
        bottom = [field[r] for r in range(rows - 4, rows)] + [after[0], after[1]]
        for p, done in ((0, top), (pairs - 1, bottom)):
            for _ in range(2):
                done = step(done, along_x, along_y)
            put(out_ref, owner_ref[0, level * pairs + p], done, width)
        return carry

    lax.fori_loop(0, levels, one, 0)


def dot(a, b):
    return jnp.dot(a, b, preferred_element_type=F32)


def dot_t(a, b):
    return lax.dot_general(a, b, (((1,), (1,)), ((), ())), preferred_element_type=F32)


def thirds(row):
    first = row.astype(BF16)
    rest = row - first.astype(F32)
    second = rest.astype(BF16)
    third = (rest - second.astype(F32)).astype(BF16)
    which = lax.broadcasted_iota(jnp.int32, (16, row.shape[1]), 0)
    parts = jnp.where(
        which == 0,
        first.astype(F32),
        jnp.where(which == 1, second.astype(F32), jnp.where(which == 2, third.astype(F32), 0.0)),
    )
    return parts.astype(BF16)


def whole(parts):
    return (parts[2:3] + parts[1:2]) + parts[0:1]


def analysis_kernel(cells_ref, bins_ref, values_ref, x_ref, out_ref, y_ref, z_ref, f_ref):
    members, tile = x_ref.shape
    obs = cells_ref.shape[1]
    ensemble = x_ref[...].astype(F32)
    average = jnp.sum(ensemble, axis=0, keepdims=True) * (1.0 / members)
    spread = (ensemble - average).astype(BF16)
    cells = cells_ref[...]
    chosen = lax.broadcasted_iota(jnp.int32, (tile, obs), 0) == cells
    chosen = jnp.where(chosen, 1.0, 0.0).astype(BF16)
    picked = dot(spread, chosen).astype(BF16)
    innovation = values_ref[...] - whole(dot(thirds(average), chosen))
    weights = jnp.exp(-0.5 * (loc_step * bins_ref[...].astype(F32)) ** 2)
    scaled = (picked.astype(F32) * weights).astype(BF16)
    diagonal = lax.broadcasted_iota(jnp.int32, (members, members), 0) == lax.broadcasted_iota(
        jnp.int32, (members, members), 1
    )
    matrix = dot_t(scaled, picked) + jnp.where(diagonal, (members - 1) / inflation, 0.0)
    sums = jnp.sum(jnp.abs(matrix), axis=0, keepdims=True)
    norm_total = jnp.max(sums, axis=1, keepdims=True)
    current = (matrix / norm_total).astype(BF16)
    eye = jnp.where(diagonal, 1.5, 0.0)
    y_ref[...] = current
    first = (eye - 0.5 * current.astype(F32)).astype(BF16)
    z_ref[...] = first
    y_ref[...] = dot(first, current).astype(BF16)

    def factor():
        product = dot(y_ref[...], z_ref[...])
        on = lax.broadcasted_iota(jnp.int32, (members, members), 0) == lax.broadcasted_iota(
            jnp.int32, (members, members), 1
        )
        f_ref[...] = (jnp.where(on, 1.5, 0.0) - 0.5 * product).astype(BF16)

    def sweep(_, carry):
        factor()
        y_ref[...] = dot(f_ref[...], y_ref[...]).astype(BF16)
        z_ref[...] = dot(z_ref[...], f_ref[...]).astype(BF16)
        return carry

    lax.fori_loop(0, STEPS - 2, sweep, 0)
    factor()
    root = dot(z_ref[...], f_ref[...]).astype(BF16)
    forcing = whole(dot_t(thirds(weights * innovation), picked))
    inner = whole(dot(thirds(forcing), root))
    shift = whole(dot(thirds(inner), root)) / norm_total
    transform = (jnp.sqrt((members - 1) / norm_total) * root.astype(F32) + shift).astype(BF16)
    out_ref[...] = (average + dot(transform, spread)).astype(BF16)


def restore_kernel(owner_ref, x_ref, out_ref):
    members, levels, rows, width = out_ref.shape
    pairs = rows // 2

    def one(level, carry):
        tiles = [x_ref[owner_ref[0, level * pairs + p]].astype(F32) for p in range(pairs)]
        field = jnp.stack([t[:, k * width : (k + 1) * width] for t in tiles for k in range(2)])
        out_ref[:, level] = jnp.swapaxes(field, 0, 1).astype(BF16)
        return carry

    lax.fori_loop(0, levels, one, 0)


def call(kernel, out, in_specs, flops, moved, **more):
    return pl.pallas_call(
        kernel,
        out_shape=out,
        in_specs=in_specs,
        out_specs=jax.tree.map(lambda _: VMEM, out),
        compiler_params=PARAMS,
        cost_estimate=pl.CostEstimate(flops=flops, bytes_accessed=moved, transcendentals=0),
        **more,
    )


def body(prior_sample, prior_velocity, obs_cells, obs_bins, obs_values, tile_owner):
    members, levels, rows, width = prior_sample.shape
    slots = tile_owner.shape[1]
    edge = jax.ShapeDtypeStruct((levels, 2, members, width), BF16)
    low, high = call(edges_kernel, (edge, edge), [VMEM], 10**5, 10**6)(prior_sample)
    count = lax.axis_size("dom")
    up = [(i, (i + 1) % count) for i in range(count)]
    before = lax.ppermute(high, "dom", up)
    after = lax.ppermute(low, "dom", [(t, s) for s, t in up])
    pieces = jax.ShapeDtypeStruct((slots, members, 2 * width), BF16)
    partial = call(interior_kernel, pieces, [SMEM, VMEM, VMEM], 10**7, 2 * 10**6)(
        tile_owner, prior_velocity, prior_sample
    )
    outgoing = call(
        outer_kernel,
        pieces,
        [SMEM, VMEM, VMEM, VMEM, VMEM, VMEM],
        10**7,
        10**6,
    )(tile_owner, prior_velocity, prior_sample, before, after, partial)
    received = lax.all_to_all(outgoing, MEM, split_axis=0, concat_axis=0, tiled=True)
    total = slots * members
    square = pltpu.VMEM((total, total), BF16)
    updated = call(
        analysis_kernel,
        jax.ShapeDtypeStruct((total, 2 * width), BF16),
        [VMEM] * 4,
        4 * 10**9,
        2 * 10**6,
        scratch_shapes=[square] * 3,
    )(obs_cells[0], obs_bins[0], obs_values[0], received.reshape(total, 2 * width))
    results = updated.reshape(slots, members, 2 * width)
    returned = lax.all_to_all(results, MEM, split_axis=0, concat_axis=0, tiled=True)
    return call(
        restore_kernel,
        jax.ShapeDtypeStruct(prior_sample.shape, BF16),
        [SMEM, VMEM],
        10**6,
        10**6,
    )(tile_owner, returned)


def solution(mesh):
    split = Mesh(
        mesh.devices.reshape(8, 4, 2, mesh.shape["dom"]), ("mem_0", "mem_1", "mem_2", "dom")
    )
    in_specs = (
        P(MEM, None, "dom", None),
        P(),
        P("dom", MEM, None),
        P("dom", MEM, None),
        P("dom", MEM, None),
        P("dom", None),
    )
    out_specs = P(MEM, None, "dom", None)
    return jax.shard_map(body, mesh=split, in_specs=in_specs, out_specs=out_specs, check_vma=False)
```

```python
import jax
import jax.numpy as jnp
from jax import lax
from jax.experimental import pallas as pl
from jax.experimental.pallas import tpu as pltpu
from jax.sharding import Mesh
from jax.sharding import PartitionSpec as P

STEPS = 5
MEM = ("mem_0", "mem_1", "mem_2")

advect_coef = 0.15
diffuse_coef = 0.15
loc_step = 0.35
inflation = 1.1

F32 = jnp.float32
BF16 = jnp.bfloat16
VMEM = pl.BlockSpec(memory_space=pltpu.VMEM)
SMEM = pl.BlockSpec(memory_space=pltpu.SMEM)
PARAMS = pltpu.CompilerParams(vmem_limit_bytes=48 * 1024 * 1024)


def rows_first(block):
    return jnp.swapaxes(block.astype(F32), 0, 1)


def step(rows, along_x, along_y):
    width = rows[0].shape[-1]
    below, above, inner = [], [], []
    last = len(rows) - 1
    for r, v in enumerate(rows):
        half = 0.5 * v
        flux_y = (along_y + half) * v
        below.append(v - flux_y if r >= 2 else None)
        above.append(v + flux_y if r <= last - 2 else None)
        if 1 <= r <= last - 1:
            flux_x = (along_x + half) * v
            east = pltpu.roll(v - flux_x, width - 1, axis=1)
            west = pltpu.roll(v + flux_x, 1, axis=1)
            inner.append((east + west) - 4.0 * v)
        else:
            inner.append(None)
    return [
        rows[r] + advect_coef * (inner[r] + (below[r + 1] + above[r - 1]))
        for r in range(1, last)
    ]


def edges_kernel(x_ref, in_pair_ref, across_ref):
    levels, rows = x_ref.shape[1], x_ref.shape[2]
    even = lax.rem(lax.axis_index("dom"), 2) == 0

    def send(low_ref, high_ref):
        for level in range(levels):
            block = x_ref[:, level]
            low_ref[level] = rows_first(block[:, 0:2]).astype(BF16)
            high_ref[level] = rows_first(block[:, rows - 2 : rows]).astype(BF16)

    @pl.when(even)
    def _():
        send(across_ref, in_pair_ref)

    @pl.when(jnp.logical_not(even))
    def _():
        send(in_pair_ref, across_ref)


def put(out_ref, slot, rows, width):
    out_ref[slot, :, 0:width] = rows[0].astype(BF16)
    out_ref[slot, :, width : 2 * width] = rows[1].astype(BF16)


def interior(owner_ref, velocity_ref, x_ref, out_ref, first_ref):
    members, levels, rows, width = x_ref.shape
    pairs = rows // 2

    def one(level, carry):
        along_x = velocity_ref[0, pl.ds(level, 1), :]
        along_y = velocity_ref[1, pl.ds(level, 1), :]
        field = rows_first(x_ref[:, level])
        first = step([field[r] for r in range(rows)], along_x, along_y)
        for k, r in enumerate((0, 1, rows - 4, rows - 3)):
            first_ref[level, k] = first[r]
        done = step(first, along_x, along_y)
        for p in range(1, pairs - 1):
            put(out_ref, owner_ref[0, level * pairs + p], done[2 * p - 2 : 2 * p], width)
        return carry

    lax.fori_loop(0, levels, one, 0)


def interior_kernel(
    owner_ref, velocity_ref, x_ref, cells_ref, bins_ref, values_ref,
    out_ref, first_ref, chosen_ref, weights_ref, observed_ref,
):
    tile, obs = chosen_ref.shape
    rows = lax.broadcasted_iota(jnp.int32, (tile, obs), 0)
    chosen_ref[...] = jnp.where(rows == cells_ref[...], 1.0, 0.0).astype(BF16)
    weights_ref[...] = jnp.exp(-0.5 * (loc_step * bins_ref[...].astype(F32)) ** 2)
    observed_ref[...] = values_ref[...]

    @pl.when(lax.axis_index("dom") != lax.axis_size("dom") - 1)
    def _():
        interior(owner_ref, velocity_ref, x_ref, out_ref, first_ref)


def outer_kernel(
    owner_ref, velocity_ref, x_ref, in_pair_ref, across_ref, got_across_ref, got_pair_ref, got_last_ref,
    partial_ref, kept_ref, out_ref, first_ref,
):
    members, levels, rows, width = x_ref.shape
    pairs = rows // 2
    me, count = lax.axis_index("dom"), lax.axis_size("dom")
    late = me == count - 1

    @pl.when(late)
    def _():
        interior(owner_ref, velocity_ref, x_ref, out_ref, first_ref)

    @pl.when(jnp.logical_not(late))
    def _():
        out_ref[...] = partial_ref[...]
        first_ref[...] = kept_ref[...]

    def finish(before_ref, low_ref, high_ref, after_ref):
        def one(level, carry):
            along_x = velocity_ref[0, pl.ds(level, 1), :]
            along_y = velocity_ref[1, pl.ds(level, 1), :]

            def pair_of(ref):
                both = ref[level].astype(F32)
                return [both[0], both[1]]

            top = step(pair_of(before_ref) + pair_of(low_ref), along_x, along_y)
            top = step(top + [first_ref[level, 0], first_ref[level, 1]], along_x, along_y)
            put(out_ref, owner_ref[0, level * pairs], top, width)
            end = step(pair_of(high_ref) + pair_of(after_ref), along_x, along_y)
            end = step([first_ref[level, 2], first_ref[level, 3]] + end, along_x, along_y)
            put(out_ref, owner_ref[0, level * pairs + pairs - 1], end, width)
            return carry

        lax.fori_loop(0, levels, one, 0)

    even = lax.rem(me, 2) == 0
    ending = me >= count - 2
    for is_even in (True, False):
        for is_ending in (True, False):
            got_ref = got_last_ref if is_ending else got_pair_ref

            @pl.when(jnp.logical_and(even == is_even, ending == is_ending))
            def _():
                if is_even:
                    finish(got_across_ref, across_ref, in_pair_ref, got_ref)
                else:
                    finish(got_ref, in_pair_ref, across_ref, got_across_ref)


def dot(a, b):
    return jnp.dot(a, b, preferred_element_type=F32)


def dot_t(a, b):
    return lax.dot_general(a, b, (((1,), (1,)), ((), ())), preferred_element_type=F32)


def split(x):
    high = x.astype(BF16)
    return high, (x - high.astype(F32)).astype(BF16)


def dot3(a, b):
    a_high, a_low = split(a)
    b_high, b_low = split(b)
    return dot(a_high, b_high) + (dot(a_high, b_low) + dot(a_low, b_high))


def thirds(row):
    first = row.astype(BF16).astype(F32)
    second = (row - first).astype(BF16).astype(F32)
    third = (row - first) - second
    which = lax.broadcasted_iota(jnp.int32, (16, row.shape[1]), 0)
    parts = jnp.where(which == 0, first, jnp.where(which == 1, second, jnp.where(which == 2, third, 0.0)))
    return parts.astype(BF16)


def whole(parts):
    return (parts[2:3] + parts[1:2]) + parts[0:1]


def analysis_kernel(chosen_ref, weights_ref, values_ref, x_ref, out_ref):
    members, tile = x_ref.shape
    obs = chosen_ref.shape[1]
    ensemble = x_ref[...].astype(F32)
    average = jnp.sum(ensemble, axis=0, keepdims=True) * (1.0 / members)
    spread = (ensemble - average).astype(BF16)
    chosen = chosen_ref[...]
    weights = weights_ref[...]
    exact = dot(spread, chosen)
    picked = exact.astype(BF16)
    scaled = (exact * weights).astype(BF16)
    across = exact.T.astype(BF16)
    matrix = dot_t(scaled, picked)
    diagonal = lax.broadcasted_iota(jnp.int32, (members, members), 0) == lax.broadcasted_iota(
        jnp.int32, (members, members), 1
    )
    ridge = (members - 1) / inflation
    matrix = jnp.abs(matrix + jnp.where(diagonal, ridge, 0.0))
    norm_total = jnp.max(jnp.sum(matrix, axis=0, keepdims=True), axis=1, keepdims=True)
    over = 1.0 / norm_total
    gram = dot(across, spread)
    innovation = values_ref[...] - whole(dot(thirds(average), chosen))

    eye = jnp.where(
        lax.broadcasted_iota(jnp.int32, (obs, obs), 0) == lax.broadcasted_iota(jnp.int32, (obs, obs), 1), 1.0, 0.0
    )
    y_a = ridge * over
    y_c = eye
    y_small = y_a * eye + dot(across, scaled) * over
    z_a = 1.5 - 0.5 * y_a
    z_c = -0.5 * y_c
    z_small = 1.5 * eye - 0.5 * y_small
    f_a, f_c, f_small = z_a, z_c, z_small
    both = dot3(y_small, jnp.concatenate([f_small, f_c], axis=1))
    y_c = both[:, obs:] + f_a * y_c
    y_small = both[:, :obs]
    y_a = y_a * f_a
    for sweep in range(1, STEPS):
        both = dot3(z_small, jnp.concatenate([y_small, y_c], axis=1))
        f_small = 1.5 * eye - 0.5 * both[:, :obs]
        f_c = -0.5 * (both[:, obs:] + y_a * z_c)
        f_a = 1.5 - 0.5 * (z_a * y_a)
        right = jnp.concatenate([f_small, f_c], axis=1)
        if sweep + 1 < STEPS:
            both = dot3(jnp.concatenate([z_small, y_small], axis=0), right)
            y_c = both[obs:, obs:] + f_a * y_c
            y_small = both[obs:, :obs]
            y_a = y_a * f_a
        else:
            both = dot3(z_small, right)
        z_c = both[:obs, obs:] + f_a * z_c
        z_small = both[:obs, :obs]
        z_a = z_a * f_a

    scale = jnp.sqrt((members - 1) * over)
    line = jnp.broadcast_to(weights * innovation, (16, obs))
    line = dot3(dot3(line, z_small), z_small) * over
    mixed = dot3(jnp.concatenate([z_c * (scale * over), line], axis=0), gram)
    high, low = split(mixed[:obs])
    rest = dot(scaled, high) + dot(scaled, low)
    base = average + mixed[obs : obs + 1]
    out_ref[...] = (base + ((scale * z_a) * spread.astype(F32) + rest)).astype(BF16)


def restore_kernel(owner_ref, x_ref, out_ref, held_ref, sent):
    members, levels, rows, width = held_ref.shape
    pairs = rows // 2

    def copy(level):
        return pltpu.make_async_copy(held_ref.at[:, level], out_ref.at[:, level], sent.at[level])

    for level in range(levels):
        tiles = [x_ref[owner_ref[0, level * pairs + p]].astype(F32) for p in range(pairs)]
        field = jnp.stack([t[:, k * width : (k + 1) * width] for t in tiles for k in range(2)])
        held_ref[:, level] = jnp.swapaxes(field, 0, 1).astype(BF16)
        copy(level).start()
    for level in range(levels):
        copy(level).wait()


def call(kernel, out, in_specs, flops, moved, out_specs=None, **more):
    return pl.pallas_call(
        kernel,
        out_shape=out,
        in_specs=in_specs,
        out_specs=jax.tree.map(lambda _: VMEM, out) if out_specs is None else out_specs,
        compiler_params=PARAMS,
        cost_estimate=pl.CostEstimate(flops=flops, bytes_accessed=moved, transcendentals=0),
        **more,
    )


def advected(prior_sample, prior_velocity, obs_cells, obs_bins, obs_values, tile_owner):
    members, levels, rows, width = prior_sample.shape
    slots, obs = tile_owner.shape[1], obs_cells.shape[2]
    tile = 2 * width
    shape = jax.ShapeDtypeStruct
    edge = shape((levels, 2, members, width), BF16)
    in_pair, across = call(edges_kernel, (edge, edge), [VMEM], 10**5, 10**6)(prior_sample)
    count = lax.axis_size("dom")
    swaps = [(i, i ^ 1) for i in range(count)]
    got_pair = lax.ppermute(in_pair, "dom", swaps[:-2])
    pieces = shape((slots, members, tile), BF16)
    first = shape((levels, 4, members, width), F32)
    partial, kept, chosen, weights, values = call(
        interior_kernel,
        (pieces, first, shape((tile, obs), BF16), shape((1, obs), F32), shape((1, obs), F32)),
        [SMEM] + [VMEM] * 5,
        10**7,
        2 * 10**6,
    )(tile_owner, prior_velocity, prior_sample, obs_cells[0], obs_bins[0], obs_values[0])
    ready, in_pair, partial = lax.optimization_barrier((across, in_pair, partial))
    got_across = lax.ppermute(
        ready, "dom", [(i, (i + 1 if i % 2 else i - 1) % count) for i in range(count)]
    )
    got_last = lax.ppermute(in_pair, "dom", swaps[-2:])
    outgoing = call(
        outer_kernel,
        pieces,
        [SMEM] + [VMEM] * 9,
        10**7,
        10**6,
        scratch_shapes=[pltpu.VMEM(first.shape, F32)],
    )(
        tile_owner, prior_velocity, prior_sample, in_pair, across, got_across, got_pair, got_last,
        partial, kept,
    )
    return outgoing, chosen, weights, values


def body(prior_sample, prior_velocity, obs_cells, obs_bins, obs_values, tile_owner):
    outgoing, chosen, weights, values = advected(
        prior_sample, prior_velocity, obs_cells, obs_bins, obs_values, tile_owner
    )
    slots, members, tile = outgoing.shape
    total = slots * members
    received = lax.all_to_all(outgoing, MEM, split_axis=0, concat_axis=0, tiled=True)
    updated = analyse(chosen, weights, values, received.reshape(total, tile))
    results = updated.reshape(slots, members, tile)
    returned = lax.all_to_all(results, MEM, split_axis=0, concat_axis=0, tiled=True)
    return restored(tile_owner, returned, prior_sample.shape)


def analyse(chosen, weights, values, ensemble):
    out = jax.ShapeDtypeStruct(ensemble.shape, BF16)
    return call(analysis_kernel, out, [VMEM] * 4, 10**9, 2 * 10**6)(chosen, weights, values, ensemble)


def restored(tile_owner, returned, shape):
    return call(
        restore_kernel,
        jax.ShapeDtypeStruct(shape, BF16),
        [SMEM, VMEM],
        10**6,
        10**6,
        out_specs=pl.BlockSpec(memory_space=pl.ANY),
        scratch_shapes=[pltpu.VMEM(shape, BF16), pltpu.SemaphoreType.DMA((shape[1],))],
    )(tile_owner, returned)


def solution(mesh):
    split = Mesh(
        mesh.devices.reshape(8, 4, 2, mesh.shape["dom"]), ("mem_0", "mem_1", "mem_2", "dom")
    )
    in_specs = (
        P(MEM, None, "dom", None),
        P(),
        P("dom", MEM, None),
        P("dom", MEM, None),
        P("dom", MEM, None),
        P("dom", None),
    )
    out_specs = P(MEM, None, "dom", None)
    return jax.shard_map(body, mesh=split, in_specs=in_specs, out_specs=out_specs, check_vma=False)
```

```python
import jax
import jax.numpy as jnp
from jax import lax
from jax.experimental import pallas as pl
from jax.experimental.pallas import tpu as pltpu
from jax.sharding import Mesh
from jax.sharding import PartitionSpec as P

STEPS = 5
MEM = ("mem_0", "mem_1", "mem_2")

advect_coef = 0.15
diffuse_coef = 0.15
loc_step = 0.35
inflation = 1.1

F32 = jnp.float32
BF16 = jnp.bfloat16
VMEM = pl.BlockSpec(memory_space=pltpu.VMEM)
SMEM = pl.BlockSpec(memory_space=pltpu.SMEM)
PARAMS = pltpu.CompilerParams(vmem_limit_bytes=48 * 1024 * 1024)


def rows_first(block):
    return jnp.swapaxes(block.astype(F32), 0, 1)


def step(rows, along_x, along_y):
    width = rows[0].shape[-1]
    below, above, inner = [], [], []
    last = len(rows) - 1
    for r, v in enumerate(rows):
        half = 0.5 * v
        flux_y = (along_y + half) * v
        below.append(v - flux_y if r >= 2 else None)
        above.append(v + flux_y if r <= last - 2 else None)
        if 1 <= r <= last - 1:
            flux_x = (along_x + half) * v
            east = pltpu.roll(v - flux_x, width - 1, axis=1)
            west = pltpu.roll(v + flux_x, 1, axis=1)
            inner.append((east + west) - 4.0 * v)
        else:
            inner.append(None)
    return [
        rows[r] + advect_coef * (inner[r] + (below[r + 1] + above[r - 1]))
        for r in range(1, last)
    ]


def edges_kernel(x_ref, out_ref, in_pair_ref, across_ref):
    out_ref[...] = x_ref[...]
    levels, rows = x_ref.shape[1], x_ref.shape[2]
    even = lax.rem(lax.axis_index("dom"), 2) == 0

    def send(low_ref, high_ref):
        for level in range(levels):
            block = x_ref[:, level]
            low_ref[level] = rows_first(block[:, 0:2]).astype(BF16)
            high_ref[level] = rows_first(block[:, rows - 2 : rows]).astype(BF16)

    @pl.when(even)
    def _():
        send(across_ref, in_pair_ref)

    @pl.when(jnp.logical_not(even))
    def _():
        send(in_pair_ref, across_ref)


def put(out_ref, slot, rows, width):
    out_ref[slot, :, 0:width] = rows[0].astype(BF16)
    out_ref[slot, :, width : 2 * width] = rows[1].astype(BF16)


def interior(owner_ref, velocity_ref, x_ref, out_ref, first_ref):
    members, levels, rows, width = x_ref.shape
    pairs = rows // 2

    def one(level, carry):
        along_x = velocity_ref[0, pl.ds(level, 1), :]
        along_y = velocity_ref[1, pl.ds(level, 1), :]
        field = rows_first(x_ref[:, level])
        first = step([field[r] for r in range(rows)], along_x, along_y)
        for k, r in enumerate((0, 1, rows - 4, rows - 3)):
            first_ref[level, k] = first[r]
        done = step(first, along_x, along_y)
        for p in range(1, pairs - 1):
            put(out_ref, owner_ref[0, level * pairs + p], done[2 * p - 2 : 2 * p], width)
        return carry

    lax.fori_loop(0, levels, one, 0, unroll=2)


def prepare(cells_ref, bins_ref, values_ref, chosen_ref, weights_ref, observed_ref):
    tile, obs = chosen_ref.shape
    rows = lax.broadcasted_iota(jnp.int32, (tile, obs), 0)
    chosen_ref[...] = jnp.where(rows == cells_ref[...], 1.0, 0.0).astype(BF16)
    weights_ref[...] = jnp.exp(-0.5 * (loc_step * bins_ref[...].astype(F32)) ** 2)
    observed_ref[...] = values_ref[...]


def interior_kernel(
    owner_ref, velocity_ref, x_ref, cells_ref, bins_ref, values_ref,
    out_ref, first_ref, chosen_ref, weights_ref, observed_ref,
):
    @pl.when(lax.axis_index("dom") != lax.axis_size("dom") - 1)
    def _():
        interior(owner_ref, velocity_ref, x_ref, out_ref, first_ref)
        prepare(cells_ref, bins_ref, values_ref, chosen_ref, weights_ref, observed_ref)


def outer_kernel(
    owner_ref, velocity_ref, x_ref, cells_ref, bins_ref, values_ref,
    in_pair_ref, across_ref, got_across_ref, got_pair_ref, got_last_ref,
    partial_ref, kept_ref, ready_ref, weight_ref, value_ref,
    out_ref, chosen_ref, weights_ref, observed_ref, first_ref,
):
    members, levels, rows, width = x_ref.shape
    pairs = rows // 2
    me, count = lax.axis_index("dom"), lax.axis_size("dom")
    late = me == count - 1

    @pl.when(late)
    def _():
        interior(owner_ref, velocity_ref, x_ref, out_ref, first_ref)
        prepare(cells_ref, bins_ref, values_ref, chosen_ref, weights_ref, observed_ref)

    @pl.when(jnp.logical_not(late))
    def _():
        out_ref[...] = partial_ref[...]
        first_ref[...] = kept_ref[...]
        chosen_ref[...] = ready_ref[...]
        weights_ref[...] = weight_ref[...]
        observed_ref[...] = value_ref[...]

    shape = (members, width)
    even = jnp.broadcast_to(lax.rem(me, 2), shape) == 0
    ending = jnp.broadcast_to(me, shape) >= count - 2

    for level in range(levels):
        along_x = velocity_ref[0, level : level + 1, :]
        along_y = velocity_ref[1, level : level + 1, :]
        low, high, before, after = [], [], [], []
        for k in range(2):
            pair = in_pair_ref[level, k].astype(F32)
            other = across_ref[level, k].astype(F32)
            low.append(jnp.where(even, other, pair))
            high.append(jnp.where(even, pair, other))
            pair = jnp.where(ending, got_last_ref[level, k].astype(F32), got_pair_ref[level, k].astype(F32))
            other = got_across_ref[level, k].astype(F32)
            before.append(jnp.where(even, other, pair))
            after.append(jnp.where(even, pair, other))
        top = step(before + low, along_x, along_y)
        top = step(top + [first_ref[level, 0], first_ref[level, 1]], along_x, along_y)
        put(out_ref, owner_ref[0, level * pairs], top, width)
        end = step(high + after, along_x, along_y)
        end = step([first_ref[level, 2], first_ref[level, 3]] + end, along_x, along_y)
        put(out_ref, owner_ref[0, level * pairs + pairs - 1], end, width)


def dot(a, b):
    return jnp.dot(a, b, preferred_element_type=F32)


def dot_t(a, b):
    return lax.dot_general(a, b, (((1,), (1,)), ((), ())), preferred_element_type=F32)


def split(x):
    high = x.astype(BF16)
    return high, (x - high.astype(F32)).astype(BF16)


def dot3(a, b):
    a_high, a_low = split(a)
    b_high, b_low = split(b)
    return dot(
        jnp.concatenate([a_low, a_high, a_high], axis=1),
        jnp.concatenate([b_high, b_low, b_high], axis=0),
    )


def thirds(row):
    first = row.astype(BF16).astype(F32)
    second = (row - first).astype(BF16).astype(F32)
    third = (row - first) - second
    which = lax.broadcasted_iota(jnp.int32, (16, row.shape[1]), 0)
    parts = jnp.where(which == 0, first, jnp.where(which == 1, second, jnp.where(which == 2, third, 0.0)))
    return parts.astype(BF16)


def whole(parts):
    return (parts[2:3] + parts[1:2]) + parts[0:1]


def analysis_kernel(chosen_ref, weights_ref, values_ref, x_ref, out_ref):
    members, tile = x_ref.shape
    obs = chosen_ref.shape[1]
    ensemble = x_ref[...].astype(F32)
    average = jnp.sum(ensemble, axis=0, keepdims=True) * (1.0 / members)
    spread = (ensemble - average).astype(BF16)
    chosen = chosen_ref[...]
    weights = weights_ref[...]
    exact = dot(spread, chosen)
    picked = exact.astype(BF16)
    scaled = (exact * weights).astype(BF16)
    across = exact.T.astype(BF16)
    matrix = dot_t(scaled, picked)
    diagonal = lax.broadcasted_iota(jnp.int32, (members, members), 0) == lax.broadcasted_iota(
        jnp.int32, (members, members), 1
    )
    ridge = (members - 1) / inflation
    matrix = jnp.abs(matrix + jnp.where(diagonal, ridge, 0.0))
    norm_total = jnp.max(jnp.sum(matrix, axis=0, keepdims=True), axis=1, keepdims=True)
    over = 1.0 / norm_total
    gram = dot(across, spread)
    innovation = values_ref[...] - whole(dot(thirds(average), chosen))

    eye = jnp.where(
        lax.broadcasted_iota(jnp.int32, (obs, obs), 0) == lax.broadcasted_iota(jnp.int32, (obs, obs), 1), 1.0, 0.0
    )
    y_a = ridge * over
    y_c = eye
    y_small = y_a * eye + dot(across, scaled) * over
    z_a = 1.5 - 0.5 * y_a
    z_c = -0.5 * y_c
    z_small = 1.5 * eye - 0.5 * y_small
    f_a, f_c, f_small = z_a, z_c, z_small
    both = dot3(y_small, jnp.concatenate([f_small, f_c], axis=1))
    y_c = both[:, obs:] + f_a * y_c
    y_small = both[:, :obs]
    y_a = y_a * f_a
    for sweep in range(1, STEPS):
        both = dot3(z_small, jnp.concatenate([y_small, y_c], axis=1))
        f_small = 1.5 * eye - 0.5 * both[:, :obs]
        f_c = -0.5 * (both[:, obs:] + y_a * z_c)
        f_a = 1.5 - 0.5 * (z_a * y_a)
        right = jnp.concatenate([f_small, f_c], axis=1)
        if sweep + 1 < STEPS:
            both = dot3(jnp.concatenate([z_small, y_small], axis=0), right)
            y_c = both[obs:, obs:] + f_a * y_c
            y_small = both[obs:, :obs]
            y_a = y_a * f_a
        else:
            both = dot3(z_small, right)
        z_c = both[:obs, obs:] + f_a * z_c
        z_small = both[:obs, :obs]
        z_a = z_a * f_a

    scale = jnp.sqrt((members - 1) * over)
    line = jnp.broadcast_to(weights * innovation, (16, obs))
    line = dot3(dot3(line, z_small), z_small) * over
    mixed = dot3(jnp.concatenate([z_c * (scale * over), line], axis=0), gram)
    high, low = split(mixed[:obs])
    rest = dot(scaled, high) + dot(scaled, low)
    base = average + mixed[obs : obs + 1]
    out_ref[...] = (base + ((scale * z_a) * spread.astype(F32) + rest)).astype(BF16)


def restore_kernel(owner_ref, x_ref, out_ref, held_ref, sent):
    members, levels, rows, width = held_ref.shape
    pairs = rows // 2

    def copy(level):
        return pltpu.make_async_copy(held_ref.at[:, level], out_ref.at[:, level], sent.at[level])

    for level in range(levels):
        tiles = [x_ref[owner_ref[0, level * pairs + p]].astype(F32) for p in range(pairs)]
        field = jnp.stack([t[:, k * width : (k + 1) * width] for t in tiles for k in range(2)])
        held_ref[:, level] = jnp.swapaxes(field, 0, 1).astype(BF16)
        copy(level).start()
    for level in range(levels):
        copy(level).wait()


def call(kernel, out, in_specs, flops, moved, out_specs=None, **more):
    return pl.pallas_call(
        kernel,
        out_shape=out,
        in_specs=in_specs,
        out_specs=jax.tree.map(lambda _: VMEM, out) if out_specs is None else out_specs,
        compiler_params=PARAMS,
        cost_estimate=pl.CostEstimate(flops=flops, bytes_accessed=moved, transcendentals=0),
        **more,
    )


def advected(prior_sample, prior_velocity, obs_cells, obs_bins, obs_values, tile_owner):
    members, levels, rows, width = prior_sample.shape
    slots, obs = tile_owner.shape[1], obs_cells.shape[2]
    tile = 2 * width
    shape = jax.ShapeDtypeStruct
    edge = shape((levels, 2, members, width), BF16)
    sample, in_pair, across = call(
        edges_kernel, (shape(prior_sample.shape, BF16), edge, edge), [VMEM], 10**5, 10**6
    )(prior_sample)
    count = lax.axis_size("dom")
    swaps = [(i, i ^ 1) for i in range(count)]
    got_pair = lax.ppermute(in_pair, "dom", swaps[:-2])
    pieces = shape((slots, members, tile), BF16)
    first = shape((levels, 4, members, width), F32)
    prepared = (shape((tile, obs), BF16), shape((1, obs), F32), shape((1, obs), F32))
    inputs = (tile_owner, prior_velocity, sample, obs_cells[0], obs_bins[0], obs_values[0])
    done = call(
        interior_kernel, (pieces, first) + prepared, [SMEM] + [VMEM] * 5, 10**7, 2 * 10**6
    )(*inputs)
    ready, in_pair, partial = lax.optimization_barrier((across, in_pair, done[0]))
    got_across = lax.ppermute(
        ready, "dom", [(i, (i + 1 if i % 2 else i - 1) % count) for i in range(count)]
    )
    got_last = lax.ppermute(in_pair, "dom", swaps[-2:])
    outgoing, chosen, weights, observed = call(
        outer_kernel,
        (pieces,) + prepared,
        [SMEM] + [VMEM] * 15,
        10**7,
        10**6,
        scratch_shapes=[pltpu.VMEM(first.shape, F32)],
    )(*inputs, in_pair, across, got_across, got_pair, got_last, partial, *done[1:])
    return outgoing, chosen, weights, observed


def body(prior_sample, prior_velocity, obs_cells, obs_bins, obs_values, tile_owner):
    outgoing, chosen, weights, values = advected(
        prior_sample, prior_velocity, obs_cells, obs_bins, obs_values, tile_owner
    )
    slots, members, tile = outgoing.shape
    total = slots * members
    received = lax.all_to_all(outgoing, MEM, split_axis=0, concat_axis=0, tiled=True)
    updated = analyse(chosen, weights, values, received.reshape(total, tile))
    results = updated.reshape(slots, members, tile)
    returned = lax.all_to_all(results, MEM, split_axis=0, concat_axis=0, tiled=True)
    return restored(tile_owner, returned, prior_sample.shape)


def analyse(chosen, weights, values, ensemble):
    out = jax.ShapeDtypeStruct(ensemble.shape, BF16)
    return call(analysis_kernel, out, [VMEM] * 4, 10**9, 2 * 10**6)(chosen, weights, values, ensemble)


def restored(tile_owner, returned, shape):
    return call(
        restore_kernel,
        jax.ShapeDtypeStruct(shape, BF16),
        [SMEM, VMEM],
        10**6,
        10**6,
        out_specs=pl.BlockSpec(memory_space=pl.ANY),
        scratch_shapes=[pltpu.VMEM(shape, BF16), pltpu.SemaphoreType.DMA((shape[1],))],
    )(tile_owner, returned)


def solution(mesh):
    split = Mesh(
        mesh.devices.reshape(8, 4, 2, mesh.shape["dom"]), ("mem_0", "mem_1", "mem_2", "dom")
    )
    in_specs = (
        P(MEM, None, "dom", None),
        P(),
        P("dom", MEM, None),
        P("dom", MEM, None),
        P("dom", MEM, None),
        P("dom", None),
    )
    out_specs = P(MEM, None, "dom", None)
    return jax.shard_map(body, mesh=split, in_specs=in_specs, out_specs=out_specs, check_vma=False)
```

```python
import jax
import jax.numpy as jnp
from jax import lax
from jax.experimental import pallas as pl
from jax.experimental.pallas import tpu as pltpu
from jax.sharding import Mesh
from jax.sharding import PartitionSpec as P

STEPS = 5
MEM = ("mem_0", "mem_1", "mem_2")

advect_coef = 0.15
diffuse_coef = 0.15
loc_step = 0.35
inflation = 1.1

F32 = jnp.float32
BF16 = jnp.bfloat16
VMEM = pl.BlockSpec(memory_space=pltpu.VMEM)
SMEM = pl.BlockSpec(memory_space=pltpu.SMEM)
PARAMS = pltpu.CompilerParams(vmem_limit_bytes=48 * 1024 * 1024)


def rows_first(block):
    return jnp.swapaxes(block.astype(F32), 0, 1)


def step(rows, along_x, along_y):
    width = rows[0].shape[-1]
    below, above, inner = [], [], []
    last = len(rows) - 1
    for r, v in enumerate(rows):
        half = 0.5 * v
        flux_y = (along_y + half) * v
        below.append(v - flux_y if r >= 2 else None)
        above.append(v + flux_y if r <= last - 2 else None)
        if 1 <= r <= last - 1:
            flux_x = (along_x + half) * v
            east = pltpu.roll(v - flux_x, width - 1, axis=1)
            west = pltpu.roll(v + flux_x, 1, axis=1)
            inner.append((east + west) - 4.0 * v)
        else:
            inner.append(None)
    return [
        rows[r] + advect_coef * (inner[r] + (below[r + 1] + above[r - 1]))
        for r in range(1, last)
    ]


def edges_kernel(x_ref, out_ref, in_pair_ref, across_ref):
    out_ref[...] = x_ref[...]
    levels, rows = x_ref.shape[1], x_ref.shape[2]
    even = lax.rem(lax.axis_index("dom"), 2) == 0

    def send(low_ref, high_ref):
        for level in range(levels):
            block = x_ref[:, level]
            low_ref[level] = rows_first(block[:, 0:2]).astype(BF16)
            high_ref[level] = rows_first(block[:, rows - 2 : rows]).astype(BF16)

    @pl.when(even)
    def _():
        send(across_ref, in_pair_ref)

    @pl.when(jnp.logical_not(even))
    def _():
        send(in_pair_ref, across_ref)


def put(out_ref, slot, rows, width):
    out_ref[slot, :, 0:width] = rows[0].astype(BF16)
    out_ref[slot, :, width : 2 * width] = rows[1].astype(BF16)


def interior(slot_of, velocity_ref, x_ref, out_ref, first_ref):
    members, levels, rows, width = x_ref.shape
    pairs = rows // 2

    def one(level, carry):
        along_x = velocity_ref[0, pl.ds(level, 1), :]
        along_y = velocity_ref[1, pl.ds(level, 1), :]
        field = rows_first(x_ref[:, level])
        first = step([field[r] for r in range(rows)], along_x, along_y)
        for k, r in enumerate((0, 1, rows - 4, rows - 3)):
            first_ref[level, k] = first[r]
        done = step(first, along_x, along_y)
        for p in range(1, pairs - 1):
            put(out_ref, slot_of(level * pairs + p), done[2 * p - 2 : 2 * p], width)
        return carry

    lax.fori_loop(0, levels, one, 0, unroll=2)


def is_last():
    return lax.axis_index("dom") == lax.axis_size("dom") - 1


def in_last_pair():
    return lax.axis_index("dom") >= lax.axis_size("dom") - 2


def is_even():
    return lax.rem(lax.axis_index("dom"), 2) == 0


def interior_kernel(velocity_ref, x_ref, out_ref, first_ref):
    @pl.when(jnp.logical_not(is_last()))
    def _():
        interior(lambda tile: tile, velocity_ref, x_ref, out_ref, first_ref)


def border(at_top, owner_ref, velocity_ref, own_ref, got_ref, first_ref, out_ref):
    levels, _, members, width = own_ref.shape
    pairs = owner_ref.shape[1] // levels
    top = jnp.broadcast_to(at_top.astype(jnp.int32), (members, width)) == 1
    kept = jnp.where(at_top, 0, 2)
    place = jnp.where(at_top, 0, pairs - 1)
    for level in range(levels):
        along_x = velocity_ref[0, level : level + 1, :]
        along_y = velocity_ref[1, level : level + 1, :]
        own = [own_ref[level, k].astype(F32) for k in range(2)]
        got = [got_ref[level, k].astype(F32) for k in range(2)]
        rows = [jnp.where(top, g, o) for g, o in zip(got + own, own + got)]
        outer = step(rows, along_x, along_y)
        inner = [first_ref[level, kept + k] for k in range(2)]
        rows = [jnp.where(top, o, i) for o, i in zip(outer + inner, inner + outer)]
        put(out_ref, owner_ref[0, level * pairs + place], step(rows, along_x, along_y), width)


def between_kernel(
    owner_ref, velocity_ref, x_ref, cells_ref, bins_ref, values_ref, in_pair_ref, got_pair_ref, partial_ref, kept_ref,
    out_ref, first_ref, chosen_ref, weights_ref, observed_ref,
):
    tile, obs = chosen_ref.shape
    levels = x_ref.shape[1]
    pairs = owner_ref.shape[1] // levels

    @pl.when(is_last())
    def _():
        interior(lambda t: owner_ref[0, t], velocity_ref, x_ref, out_ref, first_ref)

    @pl.when(jnp.logical_not(is_last()))
    def _():
        for level in range(levels):
            for p in range(1, pairs - 1):
                out_ref[owner_ref[0, level * pairs + p]] = partial_ref[level * pairs + p]
        first_ref[...] = kept_ref[...]

    @pl.when(jnp.logical_not(in_last_pair()))
    def _():
        border(
            jnp.logical_not(is_even()), owner_ref, velocity_ref, in_pair_ref, got_pair_ref, first_ref, out_ref
        )

    rows = lax.broadcasted_iota(jnp.int32, (tile, obs), 0)
    chosen_ref[...] = jnp.where(rows == cells_ref[...], 1.0, 0.0).astype(BF16)
    weights_ref[...] = jnp.exp(-0.5 * (loc_step * bins_ref[...].astype(F32)) ** 2)
    observed_ref[...] = values_ref[...]


def border_kernel(
    owner_ref, velocity_ref, in_pair_ref, across_ref, got_across_ref, got_last_ref, first_ref, partial_ref, out_ref
):
    out_ref[...] = partial_ref[...]
    border(is_even(), owner_ref, velocity_ref, across_ref, got_across_ref, first_ref, out_ref)

    @pl.when(in_last_pair())
    def _():
        border(
            jnp.logical_not(is_even()), owner_ref, velocity_ref, in_pair_ref, got_last_ref, first_ref, out_ref
        )


def dot(a, b):
    return jnp.dot(a, b, preferred_element_type=F32)


def dot_t(a, b):
    return lax.dot_general(a, b, (((1,), (1,)), ((), ())), preferred_element_type=F32)


def split(x):
    high = x.astype(BF16)
    return high, (x - high.astype(F32)).astype(BF16)


def dot3(a, b):
    a_high, a_low = split(a)
    b_high, b_low = split(b)
    return dot(
        jnp.concatenate([a_low, a_high, a_high], axis=1),
        jnp.concatenate([b_high, b_low, b_high], axis=0),
    )


def thirds(row):
    first = row.astype(BF16).astype(F32)
    second = (row - first).astype(BF16).astype(F32)
    third = (row - first) - second
    which = lax.broadcasted_iota(jnp.int32, (16, row.shape[1]), 0)
    parts = jnp.where(which == 0, first, jnp.where(which == 1, second, jnp.where(which == 2, third, 0.0)))
    return parts.astype(BF16)


def whole(parts):
    return (parts[2:3] + parts[1:2]) + parts[0:1]


def analysis_kernel(chosen_ref, weights_ref, values_ref, x_ref, out_ref):
    members, tile = x_ref.shape
    obs = chosen_ref.shape[1]
    ensemble = x_ref[...].astype(F32)
    average = jnp.sum(ensemble, axis=0, keepdims=True) * (1.0 / members)
    spread = (ensemble - average).astype(BF16)
    chosen = chosen_ref[...]
    weights = weights_ref[...]
    exact = dot(spread, chosen)
    picked = exact.astype(BF16)
    scaled = (exact * weights).astype(BF16)
    across = exact.T.astype(BF16)
    ridge = (members - 1) / inflation
    sums = jnp.sum(jnp.abs(dot_t(scaled, picked)), axis=0, keepdims=True)
    norm_total = jnp.max(sums, axis=1, keepdims=True) + ridge
    over = 1.0 / norm_total
    gram = dot(across, spread)
    innovation = values_ref[...] - whole(dot(thirds(average), chosen))

    eye = jnp.where(
        lax.broadcasted_iota(jnp.int32, (obs, obs), 0) == lax.broadcasted_iota(jnp.int32, (obs, obs), 1), 1.0, 0.0
    )
    y_a = ridge * over
    y_c = eye
    y_small = y_a * eye + dot(across, scaled) * over
    z_a = 1.5 - 0.5 * y_a
    z_c = -0.5 * y_c
    z_small = 1.5 * eye - 0.5 * y_small
    f_a, f_c, f_small = z_a, z_c, z_small
    both = dot3(y_small, jnp.concatenate([f_small, f_c], axis=1))
    y_c = both[:, obs:] + f_a * y_c
    y_small = both[:, :obs]
    y_a = y_a * f_a
    for sweep in range(1, STEPS):
        both = dot3(z_small, jnp.concatenate([y_small, y_c], axis=1))
        f_small = 1.5 * eye - 0.5 * both[:, :obs]
        f_c = -0.5 * (both[:, obs:] + y_a * z_c)
        f_a = 1.5 - 0.5 * (z_a * y_a)
        right = jnp.concatenate([f_small, f_c], axis=1)
        if sweep + 1 < STEPS:
            both = dot3(jnp.concatenate([z_small, y_small], axis=0), right)
            y_c = both[obs:, obs:] + f_a * y_c
            y_small = both[obs:, :obs]
            y_a = y_a * f_a
        else:
            both = dot3(z_small, right)
        z_c = both[:obs, obs:] + f_a * z_c
        z_small = both[:obs, :obs]
        z_a = z_a * f_a

    scale = jnp.sqrt((members - 1) * over)
    line = jnp.broadcast_to(weights * innovation, (16, obs))
    line = dot3(dot3(line, z_small), z_small) * over
    mixed = dot3(jnp.concatenate([z_c * (scale * over), line], axis=0), gram)
    high, low = split(mixed[:obs])
    rest = dot(jnp.concatenate([scaled, scaled], axis=1), jnp.concatenate([low, high], axis=0))
    base = average + mixed[obs : obs + 1]
    out_ref[...] = (base + ((scale * z_a) * spread.astype(F32) + rest)).astype(BF16)


def restore_kernel(owner_ref, x_ref, out_ref, held_ref, sent):
    members, levels, rows, width = held_ref.shape
    pairs = rows // 2

    def copy(level):
        return pltpu.make_async_copy(held_ref.at[:, level], out_ref.at[:, level], sent.at[level])

    for level in range(levels):
        tiles = [x_ref[owner_ref[0, level * pairs + p]].astype(F32) for p in range(pairs)]
        field = jnp.stack([t[:, k * width : (k + 1) * width] for t in tiles for k in range(2)])
        held_ref[:, level] = jnp.swapaxes(field, 0, 1).astype(BF16)
        copy(level).start()
    for level in range(levels):
        copy(level).wait()


def call(kernel, out, in_specs, flops, moved, out_specs=None, **more):
    return pl.pallas_call(
        kernel,
        out_shape=out,
        in_specs=in_specs,
        out_specs=jax.tree.map(lambda _: VMEM, out) if out_specs is None else out_specs,
        compiler_params=PARAMS,
        cost_estimate=pl.CostEstimate(flops=flops, bytes_accessed=moved, transcendentals=0),
        **more,
    )


def advected(prior_sample, prior_velocity, obs_cells, obs_bins, obs_values, tile_owner):
    members, levels, rows, width = prior_sample.shape
    slots, obs = tile_owner.shape[1], obs_cells.shape[2]
    tile = 2 * width
    shape = jax.ShapeDtypeStruct
    edge = shape((levels, 2, members, width), BF16)
    sample, in_pair, across = call(
        edges_kernel, (shape(prior_sample.shape, BF16), edge, edge), [VMEM], 10**5, 10**6
    )(prior_sample)
    count = lax.axis_size("dom")
    swaps = [(i, i ^ 1) for i in range(count)]
    got_pair = lax.ppermute(in_pair, "dom", swaps[:-2])
    pieces = shape((slots, members, tile), BF16)
    first = shape((levels, 4, members, width), F32)
    prepared = (shape((tile, obs), BF16), shape((1, obs), F32), shape((1, obs), F32))
    partial, kept = call(interior_kernel, (pieces, first), [VMEM] * 2, 10**7, 2 * 10**6)(
        prior_velocity, sample
    )
    ready, in_pair, partial = lax.optimization_barrier((across, in_pair, partial))
    got_across = lax.ppermute(
        ready, "dom", [(i, (i + 1 if i % 2 else i - 1) % count) for i in range(count)]
    )
    got_last = lax.ppermute(in_pair, "dom", swaps[-2:])
    partial, kept, chosen, weights, observed = call(
        between_kernel, (pieces, first) + prepared, [SMEM] + [VMEM] * 9, 10**7, 2 * 10**6
    )(
        tile_owner, prior_velocity, sample, obs_cells[0], obs_bins[0], obs_values[0],
        in_pair, got_pair, partial, kept,
    )
    outgoing = call(border_kernel, pieces, [SMEM] + [VMEM] * 7, 10**6, 10**6)(
        tile_owner, prior_velocity, in_pair, across, got_across, got_last, kept, partial
    )
    return outgoing, chosen, weights, observed


def body(prior_sample, prior_velocity, obs_cells, obs_bins, obs_values, tile_owner):
    outgoing, chosen, weights, values = advected(
        prior_sample, prior_velocity, obs_cells, obs_bins, obs_values, tile_owner
    )
    slots, members, tile = outgoing.shape
    total = slots * members
    received = lax.all_to_all(outgoing, MEM, split_axis=0, concat_axis=0, tiled=True)
    updated = analyse(chosen, weights, values, received.reshape(total, tile))
    results = updated.reshape(slots, members, tile)
    returned = lax.all_to_all(results, MEM, split_axis=0, concat_axis=0, tiled=True)
    return restored(tile_owner, returned, prior_sample.shape)


def analyse(chosen, weights, values, ensemble):
    out = jax.ShapeDtypeStruct(ensemble.shape, BF16)
    return call(analysis_kernel, out, [VMEM] * 4, 10**9, 2 * 10**6)(chosen, weights, values, ensemble)


def restored(tile_owner, returned, shape):
    return call(
        restore_kernel,
        jax.ShapeDtypeStruct(shape, BF16),
        [SMEM, VMEM],
        10**6,
        10**6,
        out_specs=pl.BlockSpec(memory_space=pl.ANY),
        scratch_shapes=[pltpu.VMEM(shape, BF16), pltpu.SemaphoreType.DMA((shape[1],))],
    )(tile_owner, returned)


def solution(mesh):
    split = Mesh(
        mesh.devices.reshape(8, 4, 2, mesh.shape["dom"]), ("mem_0", "mem_1", "mem_2", "dom")
    )
    in_specs = (
        P(MEM, None, "dom", None),
        P(),
        P("dom", MEM, None),
        P("dom", MEM, None),
        P("dom", MEM, None),
        P("dom", None),
    )
    out_specs = P(MEM, None, "dom", None)
    return jax.shard_map(body, mesh=split, in_specs=in_specs, out_specs=out_specs, check_vma=False)
```

```python
import jax
import jax.numpy as jnp
from jax import lax
from jax.experimental import pallas as pl
from jax.experimental.pallas import tpu as pltpu
from jax.sharding import Mesh
from jax.sharding import PartitionSpec as P

STEPS = 5
MEM = ("mem_0", "mem_1", "mem_2")

advect_coef = 0.15
diffuse_coef = 0.15
loc_step = 0.35
inflation = 1.1

F32 = jnp.float32
BF16 = jnp.bfloat16
VMEM = pl.BlockSpec(memory_space=pltpu.VMEM)
SMEM = pl.BlockSpec(memory_space=pltpu.SMEM)
PARAMS = pltpu.CompilerParams(vmem_limit_bytes=48 * 1024 * 1024)


def rows_first(block):
    return jnp.swapaxes(block.astype(F32), 0, 1)


def step(rows, along_x, along_y):
    width = rows[0].shape[-1]
    below, above, inner = [], [], []
    last = len(rows) - 1
    for r, v in enumerate(rows):
        half = 0.5 * v
        flux_y = (along_y + half) * v
        below.append(v - flux_y if r >= 2 else None)
        above.append(v + flux_y if r <= last - 2 else None)
        if 1 <= r <= last - 1:
            flux_x = (along_x + half) * v
            east = pltpu.roll(v - flux_x, width - 1, axis=1)
            west = pltpu.roll(v + flux_x, 1, axis=1)
            inner.append((east + west) - 4.0 * v)
        else:
            inner.append(None)
    return [
        rows[r] + advect_coef * (inner[r] + (below[r + 1] + above[r - 1]))
        for r in range(1, last)
    ]


def edges_kernel(x_ref, out_ref, in_pair_ref, across_ref):
    out_ref[...] = x_ref[...]
    levels, rows = x_ref.shape[1], x_ref.shape[2]
    even = lax.rem(lax.axis_index("dom"), 2) == 0

    def send(low_ref, high_ref):
        for level in range(levels):
            block = x_ref[:, level]
            low_ref[level] = rows_first(block[:, 0:2]).astype(BF16)
            high_ref[level] = rows_first(block[:, rows - 2 : rows]).astype(BF16)

    @pl.when(even)
    def _():
        send(across_ref, in_pair_ref)

    @pl.when(jnp.logical_not(even))
    def _():
        send(in_pair_ref, across_ref)


def put(out_ref, slot, rows, width):
    out_ref[slot, :, 0:width] = rows[0].astype(BF16)
    out_ref[slot, :, width : 2 * width] = rows[1].astype(BF16)


def interior(slot_of, velocity_ref, x_ref, out_ref, first_ref):
    members, levels, rows, width = x_ref.shape
    pairs = rows // 2

    def one(level, carry):
        along_x = velocity_ref[0, pl.ds(level, 1), :]
        along_y = velocity_ref[1, pl.ds(level, 1), :]
        field = rows_first(x_ref[:, level])
        first = step([field[r] for r in range(rows)], along_x, along_y)
        for k, r in enumerate((0, 1, rows - 4, rows - 3)):
            first_ref[level, k] = first[r]
        done = step(first, along_x, along_y)
        for p in range(1, pairs - 1):
            put(out_ref, slot_of(level * pairs + p), done[2 * p - 2 : 2 * p], width)
        return carry

    lax.fori_loop(0, levels, one, 0, unroll=2)


def is_last():
    return lax.axis_index("dom") == lax.axis_size("dom") - 1


def in_last_pair():
    return lax.axis_index("dom") >= lax.axis_size("dom") - 2


def is_even():
    return lax.rem(lax.axis_index("dom"), 2) == 0


def interior_kernel(velocity_ref, x_ref, out_ref, first_ref):
    @pl.when(jnp.logical_not(is_last()))
    def _():
        interior(lambda tile: tile, velocity_ref, x_ref, out_ref, first_ref)


def border(at_top, owner_ref, velocity_ref, own_ref, got_ref, first_ref, out_ref):
    levels, _, members, width = own_ref.shape
    pairs = owner_ref.shape[1] // levels
    top = jnp.broadcast_to(at_top.astype(jnp.int32), (members, width)) == 1
    kept = jnp.where(at_top, 0, 2)
    place = jnp.where(at_top, 0, pairs - 1)
    for level in range(levels):
        along_x = velocity_ref[0, level : level + 1, :]
        along_y = velocity_ref[1, level : level + 1, :]
        own = [own_ref[level, k].astype(F32) for k in range(2)]
        got = [got_ref[level, k].astype(F32) for k in range(2)]
        rows = [jnp.where(top, g, o) for g, o in zip(got + own, own + got)]
        outer = step(rows, along_x, along_y)
        inner = [first_ref[level, kept + k] for k in range(2)]
        rows = [jnp.where(top, o, i) for o, i in zip(outer + inner, inner + outer)]
        put(out_ref, owner_ref[0, level * pairs + place], step(rows, along_x, along_y), width)


def between_kernel(
    owner_ref, velocity_ref, x_ref, in_pair_ref, got_pair_ref, partial_ref, kept_ref, out_ref, first_ref
):
    levels = x_ref.shape[1]
    pairs = owner_ref.shape[1] // levels

    @pl.when(is_last())
    def _():
        interior(lambda t: owner_ref[0, t], velocity_ref, x_ref, out_ref, first_ref)

    @pl.when(jnp.logical_not(is_last()))
    def _():
        for level in range(levels):
            for p in range(1, pairs - 1):
                out_ref[owner_ref[0, level * pairs + p]] = partial_ref[level * pairs + p]
        first_ref[...] = kept_ref[...]

    @pl.when(jnp.logical_not(in_last_pair()))
    def _():
        border(
            jnp.logical_not(is_even()), owner_ref, velocity_ref, in_pair_ref, got_pair_ref, first_ref, out_ref
        )


def border_kernel(
    owner_ref, velocity_ref, in_pair_ref, across_ref, got_across_ref, got_last_ref, first_ref, partial_ref, out_ref
):
    out_ref[...] = partial_ref[...]
    border(is_even(), owner_ref, velocity_ref, across_ref, got_across_ref, first_ref, out_ref)

    @pl.when(in_last_pair())
    def _():
        border(
            jnp.logical_not(is_even()), owner_ref, velocity_ref, in_pair_ref, got_last_ref, first_ref, out_ref
        )


def prepare_kernel(cells_ref, bins_ref, values_ref, chosen_ref, turned_ref, weights_ref, observed_ref):
    tile, obs = chosen_ref.shape
    rows = lax.broadcasted_iota(jnp.int32, (tile, obs), 0)
    chosen = jnp.where(rows == cells_ref[...], 1.0, 0.0)
    chosen_ref[...] = chosen.astype(BF16)
    turned_ref[...] = chosen.T.astype(BF16)
    weights_ref[...] = jnp.exp(-0.5 * (loc_step * bins_ref[...].astype(F32)) ** 2)
    observed_ref[...] = values_ref[...]


def dot(a, b):
    return jnp.dot(a, b, preferred_element_type=F32)


def dot_t(a, b):
    return lax.dot_general(a, b, (((1,), (1,)), ((), ())), preferred_element_type=F32)


def split(x):
    high = x.astype(BF16)
    return high, (x - high.astype(F32)).astype(BF16)


def dot3(a, b):
    a_high, a_low = split(a)
    b_high, b_low = split(b)
    return dot(
        jnp.concatenate([a_low, a_high, a_high], axis=1),
        jnp.concatenate([b_high, b_low, b_high], axis=0),
    )


def thirds(row):
    first = row.astype(BF16).astype(F32)
    second = (row - first).astype(BF16).astype(F32)
    third = (row - first) - second
    which = lax.broadcasted_iota(jnp.int32, (16, row.shape[1]), 0)
    parts = jnp.where(which == 0, first, jnp.where(which == 1, second, jnp.where(which == 2, third, 0.0)))
    return parts.astype(BF16)


def whole(parts):
    return (parts[2:3] + parts[1:2]) + parts[0:1]


def analysis_kernel(chosen_ref, turned_ref, weights_ref, values_ref, x_ref, out_ref):
    members, tile = x_ref.shape
    obs = chosen_ref.shape[1]
    ensemble = x_ref[...].astype(F32)
    average = jnp.sum(ensemble, axis=0, keepdims=True) * (1.0 / members)
    spread = (ensemble - average).astype(BF16)
    chosen = chosen_ref[...]
    weights = weights_ref[...]
    exact = dot(spread, chosen)
    picked = exact.astype(BF16)
    scaled = (exact * weights).astype(BF16)
    across = dot_t(turned_ref[...], spread).astype(BF16)
    ridge = (members - 1) / inflation
    sums = jnp.sum(jnp.abs(dot_t(scaled, picked)), axis=0, keepdims=True)
    norm_total = jnp.max(sums, axis=1, keepdims=True) + ridge
    over = 1.0 / norm_total
    gram = dot(across, spread)
    innovation = values_ref[...] - whole(dot(thirds(average), chosen))

    eye = jnp.where(
        lax.broadcasted_iota(jnp.int32, (obs, obs), 0) == lax.broadcasted_iota(jnp.int32, (obs, obs), 1), 1.0, 0.0
    )
    y_a = ridge * over
    y_c = eye
    y_small = y_a * eye + dot(across, scaled) * over
    z_a = 1.5 - 0.5 * y_a
    z_c = -0.5 * y_c
    z_small = 1.5 * eye - 0.5 * y_small
    f_a, f_c, f_small = z_a, z_c, z_small
    both = dot3(y_small, jnp.concatenate([f_small, f_c], axis=1))
    y_c = both[:, obs:] + f_a * y_c
    y_small = both[:, :obs]
    y_a = y_a * f_a
    for sweep in range(1, STEPS):
        both = dot3(z_small, jnp.concatenate([y_small, y_c], axis=1))
        f_small = 1.5 * eye - 0.5 * both[:, :obs]
        f_c = -0.5 * (both[:, obs:] + y_a * z_c)
        f_a = 1.5 - 0.5 * (z_a * y_a)
        right = jnp.concatenate([f_small, f_c], axis=1)
        if sweep + 1 < STEPS:
            both = dot3(jnp.concatenate([z_small, y_small], axis=0), right)
            y_c = both[obs:, obs:] + f_a * y_c
            y_small = both[obs:, :obs]
            y_a = y_a * f_a
        else:
            both = dot3(z_small, right)
        z_c = both[:obs, obs:] + f_a * z_c
        z_small = both[:obs, :obs]
        z_a = z_a * f_a

    scale = jnp.sqrt((members - 1) * over)
    line = dot3(jnp.broadcast_to(weights * innovation, (16, obs)), z_small) * over
    mixed = dot3(jnp.concatenate([z_c * (scale * over), z_small], axis=0), gram)
    high, low = split(mixed[:obs])
    base = average + dot3(line, mixed[obs:])[0:1]
    rest = dot(jnp.concatenate([scaled, scaled], axis=1), jnp.concatenate([low, high], axis=0))
    out_ref[...] = (base + ((scale * z_a) * spread.astype(F32) + rest)).astype(BF16)


def restore_kernel(owner_ref, x_ref, out_ref, held_ref, sent):
    members, levels, rows, width = held_ref.shape
    pairs = rows // 2

    def copy(level):
        return pltpu.make_async_copy(held_ref.at[:, level], out_ref.at[:, level], sent.at[level])

    for level in range(levels):
        tiles = [x_ref[owner_ref[0, level * pairs + p]].astype(F32) for p in range(pairs)]
        field = jnp.stack([t[:, k * width : (k + 1) * width] for t in tiles for k in range(2)])
        held_ref[:, level] = jnp.swapaxes(field, 0, 1).astype(BF16)
        copy(level).start()
    for level in range(levels):
        copy(level).wait()


def call(kernel, out, in_specs, flops, moved, out_specs=None, **more):
    return pl.pallas_call(
        kernel,
        out_shape=out,
        in_specs=in_specs,
        out_specs=jax.tree.map(lambda _: VMEM, out) if out_specs is None else out_specs,
        compiler_params=PARAMS,
        cost_estimate=pl.CostEstimate(flops=flops, bytes_accessed=moved, transcendentals=0),
        **more,
    )


def advected(prior_sample, prior_velocity, tile_owner):
    members, levels, rows, width = prior_sample.shape
    slots, tile = tile_owner.shape[1], 2 * width
    shape = jax.ShapeDtypeStruct
    edge = shape((levels, 2, members, width), BF16)
    sample, in_pair, across = call(
        edges_kernel, (shape(prior_sample.shape, BF16), edge, edge), [VMEM], 10**5, 10**6
    )(prior_sample)
    count = lax.axis_size("dom")
    swaps = [(i, i ^ 1) for i in range(count)]
    got_pair = lax.ppermute(in_pair, "dom", swaps[:-2])
    pieces = shape((slots, members, tile), BF16)
    first = shape((levels, 4, members, width), F32)
    partial, kept = call(interior_kernel, (pieces, first), [VMEM] * 2, 10**7, 2 * 10**6)(
        prior_velocity, sample
    )
    ready, in_pair, partial = lax.optimization_barrier((across, in_pair, partial))
    got_across = lax.ppermute(
        ready, "dom", [(i, (i + 1 if i % 2 else i - 1) % count) for i in range(count)]
    )
    got_last = lax.ppermute(in_pair, "dom", swaps[-2:])
    partial, kept = call(
        between_kernel, (pieces, first), [SMEM] + [VMEM] * 6, 10**7, 2 * 10**6
    )(tile_owner, prior_velocity, sample, in_pair, got_pair, partial, kept)
    return call(border_kernel, pieces, [SMEM] + [VMEM] * 7, 10**6, 10**6)(
        tile_owner, prior_velocity, in_pair, across, got_across, got_last, kept, partial
    )


def prepared(cells, bins, values, tile):
    shape = jax.ShapeDtypeStruct
    obs = cells.shape[1]
    row = shape((1, obs), F32)
    out = (shape((tile, obs), BF16), shape((obs, tile), BF16), row, row)
    return call(prepare_kernel, out, [VMEM] * 3, 10**6, 10**6)(cells, bins, values)


def body(prior_sample, prior_velocity, obs_cells, obs_bins, obs_values, tile_owner):
    outgoing = advected(prior_sample, prior_velocity, tile_owner)
    slots, members, tile = outgoing.shape
    total = slots * members
    cells, bins, values, outgoing = lax.optimization_barrier((obs_cells, obs_bins, obs_values, outgoing))
    received = lax.all_to_all(outgoing, MEM, split_axis=0, concat_axis=0, tiled=True)
    ready = prepared(cells[0], bins[0], values[0], tile)
    updated = analyse(*ready, received.reshape(total, tile))
    results = updated.reshape(slots, members, tile)
    returned = lax.all_to_all(results, MEM, split_axis=0, concat_axis=0, tiled=True)
    return restored(tile_owner, returned, prior_sample.shape)


def analyse(chosen, turned, weights, values, ensemble):
    out = jax.ShapeDtypeStruct(ensemble.shape, BF16)
    return call(analysis_kernel, out, [VMEM] * 5, 10**9, 2 * 10**6)(
        chosen, turned, weights, values, ensemble
    )


def restored(tile_owner, returned, shape):
    return call(
        restore_kernel,
        jax.ShapeDtypeStruct(shape, BF16),
        [SMEM, VMEM],
        10**6,
        10**6,
        out_specs=pl.BlockSpec(memory_space=pl.ANY),
        scratch_shapes=[pltpu.VMEM(shape, BF16), pltpu.SemaphoreType.DMA((shape[1],))],
    )(tile_owner, returned)


def solution(mesh):
    split = Mesh(
        mesh.devices.reshape(8, 4, 2, mesh.shape["dom"]), ("mem_0", "mem_1", "mem_2", "dom")
    )
    in_specs = (
        P(MEM, None, "dom", None),
        P(),
        P("dom", MEM, None),
        P("dom", MEM, None),
        P("dom", MEM, None),
        P("dom", None),
    )
    out_specs = P(MEM, None, "dom", None)
    return jax.shard_map(body, mesh=split, in_specs=in_specs, out_specs=out_specs, check_vma=False)
```

```python
import jax
import jax.numpy as jnp
from jax import lax
from jax.experimental import pallas as pl
from jax.experimental.pallas import tpu as pltpu
from jax.sharding import Mesh
from jax.sharding import PartitionSpec as P

STEPS = 5
MEM = ("mem_0", "mem_1", "mem_2")

advect_coef = 0.15
diffuse_coef = 0.15
loc_step = 0.35
inflation = 1.1

F32 = jnp.float32
BF16 = jnp.bfloat16
VMEM = pl.BlockSpec(memory_space=pltpu.VMEM)
SMEM = pl.BlockSpec(memory_space=pltpu.SMEM)
PARAMS = pltpu.CompilerParams(vmem_limit_bytes=48 * 1024 * 1024)


def rows_first(block):
    return jnp.swapaxes(block.astype(F32), 0, 1)


def step(rows, along_x, along_y):
    width = rows[0].shape[-1]
    below, above, inner = [], [], []
    last = len(rows) - 1
    for r, v in enumerate(rows):
        half = 0.5 * v
        flux_y = (along_y + half) * v
        below.append(v - flux_y if r >= 2 else None)
        above.append(v + flux_y if r <= last - 2 else None)
        if 1 <= r <= last - 1:
            flux_x = (along_x + half) * v
            east = pltpu.roll(v - flux_x, width - 1, axis=1)
            west = pltpu.roll(v + flux_x, 1, axis=1)
            inner.append((east + west) - 4.0 * v)
        else:
            inner.append(None)
    return [
        rows[r] + advect_coef * (inner[r] + (below[r + 1] + above[r - 1]))
        for r in range(1, last)
    ]


def edges_kernel(x_ref, out_ref, in_pair_ref, across_ref):
    out_ref[...] = x_ref[...]
    levels, rows = x_ref.shape[1], x_ref.shape[2]
    even = lax.rem(lax.axis_index("dom"), 2) == 0

    def send(low_ref, high_ref):
        for level in range(levels):
            block = x_ref[:, level]
            low_ref[level] = rows_first(block[:, 0:2]).astype(BF16)
            high_ref[level] = rows_first(block[:, rows - 2 : rows]).astype(BF16)

    @pl.when(even)
    def _():
        send(across_ref, in_pair_ref)

    @pl.when(jnp.logical_not(even))
    def _():
        send(in_pair_ref, across_ref)


def put(out_ref, slot, rows, width):
    out_ref[slot, :, 0:width] = rows[0].astype(BF16)
    out_ref[slot, :, width : 2 * width] = rows[1].astype(BF16)


def interior(slot_of, velocity_ref, x_ref, out_ref, first_ref):
    members, levels, rows, width = x_ref.shape
    pairs = rows // 2

    def one(level, carry):
        along_x = velocity_ref[0, pl.ds(level, 1), :]
        along_y = velocity_ref[1, pl.ds(level, 1), :]
        field = rows_first(x_ref[:, level])
        first = step([field[r] for r in range(rows)], along_x, along_y)
        for k, r in enumerate((0, 1, rows - 4, rows - 3)):
            first_ref[level, k] = first[r]
        done = step(first, along_x, along_y)
        for p in range(1, pairs - 1):
            put(out_ref, slot_of(level * pairs + p), done[2 * p - 2 : 2 * p], width)
        return carry

    lax.fori_loop(0, levels, one, 0, unroll=2)


def is_last():
    return lax.axis_index("dom") == lax.axis_size("dom") - 1


def in_last_pair():
    return lax.axis_index("dom") >= lax.axis_size("dom") - 2


def is_even():
    return lax.rem(lax.axis_index("dom"), 2) == 0


def interior_kernel(velocity_ref, x_ref, out_ref, first_ref):
    @pl.when(jnp.logical_not(is_last()))
    def _():
        interior(lambda tile: tile, velocity_ref, x_ref, out_ref, first_ref)


def border(at_top, owner_ref, velocity_ref, own_ref, got_ref, first_ref, out_ref):
    levels, _, members, width = own_ref.shape
    pairs = owner_ref.shape[1] // levels
    top = jnp.broadcast_to(at_top.astype(jnp.int32), (members, width)) == 1
    kept = jnp.where(at_top, 0, 2)
    place = jnp.where(at_top, 0, pairs - 1)
    for level in range(levels):
        along_x = velocity_ref[0, level : level + 1, :]
        along_y = velocity_ref[1, level : level + 1, :]
        own = [own_ref[level, k].astype(F32) for k in range(2)]
        got = [got_ref[level, k].astype(F32) for k in range(2)]
        rows = [jnp.where(top, g, o) for g, o in zip(got + own, own + got)]
        outer = step(rows, along_x, along_y)
        inner = [first_ref[level, kept + k] for k in range(2)]
        rows = [jnp.where(top, o, i) for o, i in zip(outer + inner, inner + outer)]
        put(out_ref, owner_ref[0, level * pairs + place], step(rows, along_x, along_y), width)


def between_kernel(
    owner_ref, velocity_ref, x_ref, cells_ref, bins_ref, values_ref, in_pair_ref, got_pair_ref, partial_ref, kept_ref,
    out_ref, first_ref, chosen_ref, weights_ref, observed_ref,
):
    tile, obs = chosen_ref.shape
    levels = x_ref.shape[1]
    pairs = owner_ref.shape[1] // levels

    @pl.when(is_last())
    def _():
        interior(lambda t: owner_ref[0, t], velocity_ref, x_ref, out_ref, first_ref)

    @pl.when(jnp.logical_not(is_last()))
    def _():
        for level in range(levels):
            for p in range(1, pairs - 1):
                out_ref[owner_ref[0, level * pairs + p]] = partial_ref[level * pairs + p]
        first_ref[...] = kept_ref[...]

    @pl.when(jnp.logical_not(in_last_pair()))
    def _():
        border(
            jnp.logical_not(is_even()), owner_ref, velocity_ref, in_pair_ref, got_pair_ref, first_ref, out_ref
        )

    rows = lax.broadcasted_iota(jnp.int32, (tile, obs), 0)
    chosen_ref[...] = jnp.where(rows == cells_ref[...], 1.0, 0.0).astype(BF16)
    weights_ref[...] = jnp.exp(-0.5 * (loc_step * bins_ref[...].astype(F32)) ** 2)
    observed_ref[...] = values_ref[...]


def border_kernel(
    slots_ref, velocity_ref, in_pair_ref, across_ref, got_across_ref, got_last_ref, first_ref, partial_ref, out_ref,
    owner_ref, arrived,
):
    slots = pltpu.make_async_copy(slots_ref, owner_ref, arrived)
    slots.start()
    out_ref[...] = partial_ref[...]
    slots.wait()
    border(is_even(), owner_ref, velocity_ref, across_ref, got_across_ref, first_ref, out_ref)

    @pl.when(in_last_pair())
    def _():
        border(
            jnp.logical_not(is_even()), owner_ref, velocity_ref, in_pair_ref, got_last_ref, first_ref, out_ref
        )


def dot(a, b):
    return jnp.dot(a, b, preferred_element_type=F32)


def dot_t(a, b):
    return lax.dot_general(a, b, (((1,), (1,)), ((), ())), preferred_element_type=F32)


def split(x):
    high = x.astype(BF16)
    return high, (x - high.astype(F32)).astype(BF16)


def dot3(a, b):
    a_high, a_low = split(a)
    b_high, b_low = split(b)
    return dot(
        jnp.concatenate([a_low, a_high, a_high], axis=1),
        jnp.concatenate([b_high, b_low, b_high], axis=0),
    )


def thirds(row):
    first = row.astype(BF16).astype(F32)
    second = (row - first).astype(BF16).astype(F32)
    third = (row - first) - second
    which = lax.broadcasted_iota(jnp.int32, (16, row.shape[1]), 0)
    parts = jnp.where(which == 0, first, jnp.where(which == 1, second, jnp.where(which == 2, third, 0.0)))
    return parts.astype(BF16)


def whole(parts):
    return (parts[2:3] + parts[1:2]) + parts[0:1]


def analysis_kernel(chosen_ref, weights_ref, values_ref, x_ref, out_ref):
    members, tile = x_ref.shape
    obs = chosen_ref.shape[1]
    ensemble = x_ref[...].astype(F32)
    average = jnp.sum(ensemble, axis=0, keepdims=True) * (1.0 / members)
    spread = (ensemble - average).astype(BF16)
    chosen = chosen_ref[...]
    weights = weights_ref[...]
    exact = dot(spread, chosen)
    picked = exact.astype(BF16)
    scaled = (exact * weights).astype(BF16)
    across = exact.T.astype(BF16)
    ridge = (members - 1) / inflation
    sums = jnp.sum(jnp.abs(dot_t(scaled, picked)), axis=0, keepdims=True)
    norm_total = jnp.max(sums, axis=1, keepdims=True) + ridge
    over = 1.0 / norm_total
    gram = dot(across, spread)
    innovation = values_ref[...] - whole(dot(thirds(average), chosen))

    eye = jnp.where(
        lax.broadcasted_iota(jnp.int32, (obs, obs), 0) == lax.broadcasted_iota(jnp.int32, (obs, obs), 1), 1.0, 0.0
    )
    w_a = ridge * over
    w_c = eye
    w_small = w_a * eye + dot(across, scaled) * over
    z_a = 1.5 - 0.5 * w_a
    z_c = -0.5 * w_c
    z_small = 1.5 * eye - 0.5 * w_small
    for sweep in range(STEPS - 1):
        right = jnp.concatenate([w_small, w_c], axis=1)
        if sweep == 0:
            both = dot3(w_small, right)
        else:
            both = dot3(jnp.concatenate([w_small, z_small], axis=0), right)
            z_c = 1.5 * z_c - 0.5 * (both[obs:, obs:] + w_a * z_c)
            z_small = 1.5 * z_small - 0.5 * both[obs:, :obs]
            z_a = z_a * (1.5 - 0.5 * w_a)
        u_small = both[:obs, :obs]
        u_c = both[:obs, obs:] + w_a * w_c
        u_a = w_a * w_a
        f_small = 2.25 * eye - 1.5 * w_small + 0.25 * u_small
        f_c = 0.25 * u_c - 1.5 * w_c
        f_a = 2.25 - 1.5 * w_a + 0.25 * u_a
        both = dot3(w_small, jnp.concatenate([f_small, f_c], axis=1))
        w_c = both[:, obs:] + f_a * w_c
        w_small = both[:, :obs]
        w_a = w_a * f_a
    both = dot3(z_small, jnp.concatenate([w_small, w_c], axis=1))
    z_c = 1.5 * z_c - 0.5 * (both[:, obs:] + w_a * z_c)
    z_small = 1.5 * z_small - 0.5 * both[:, :obs]
    z_a = z_a * (1.5 - 0.5 * w_a)

    scale = jnp.sqrt((members - 1) * over)
    line = jnp.broadcast_to(weights * innovation, (16, obs))
    line = dot3(dot3(line, z_small), z_small) * over
    mixed = dot3(jnp.concatenate([z_c * (scale * over), line], axis=0), gram)
    high, low = split(mixed[:obs])
    rest = dot(jnp.concatenate([scaled, scaled], axis=1), jnp.concatenate([low, high], axis=0))
    base = average + mixed[obs : obs + 1]
    out_ref[...] = (base + ((scale * z_a) * spread.astype(F32) + rest)).astype(BF16)


def restore_kernel(owner_ref, x_ref, out_ref, held_ref, sent):
    members, levels, rows, width = held_ref.shape
    pairs = rows // 2

    def copy(level):
        return pltpu.make_async_copy(held_ref.at[:, level], out_ref.at[:, level], sent.at[level])

    for level in range(levels):
        tiles = [x_ref[owner_ref[0, level * pairs + p]].astype(F32) for p in range(pairs)]
        field = jnp.stack([t[:, k * width : (k + 1) * width] for t in tiles for k in range(2)])
        held_ref[:, level] = jnp.swapaxes(field, 0, 1).astype(BF16)
        copy(level).start()
    for level in range(levels):
        copy(level).wait()


def call(kernel, out, in_specs, flops, moved, out_specs=None, **more):
    return pl.pallas_call(
        kernel,
        out_shape=out,
        in_specs=in_specs,
        out_specs=jax.tree.map(lambda _: VMEM, out) if out_specs is None else out_specs,
        compiler_params=PARAMS,
        cost_estimate=pl.CostEstimate(flops=flops, bytes_accessed=moved, transcendentals=0),
        **more,
    )


def advected(prior_sample, prior_velocity, obs_cells, obs_bins, obs_values, tile_owner):
    members, levels, rows, width = prior_sample.shape
    slots, obs = tile_owner.shape[1], obs_cells.shape[2]
    tile = 2 * width
    shape = jax.ShapeDtypeStruct
    edge = shape((levels, 2, members, width), BF16)
    sample, in_pair, across = call(
        edges_kernel, (shape(prior_sample.shape, BF16), edge, edge), [VMEM], 10**5, 10**6
    )(prior_sample)
    count = lax.axis_size("dom")
    swaps = [(i, i ^ 1) for i in range(count)]
    got_pair = lax.ppermute(in_pair, "dom", swaps[:-2])
    pieces = shape((slots, members, tile), BF16)
    first = shape((levels, 4, members, width), F32)
    prepared = (shape((tile, obs), BF16), shape((1, obs), F32), shape((1, obs), F32))
    partial, kept = call(interior_kernel, (pieces, first), [VMEM] * 2, 10**7, 2 * 10**6)(
        prior_velocity, sample
    )
    ready, in_pair, partial = lax.optimization_barrier((across, in_pair, partial))
    got_across = lax.ppermute(
        ready, "dom", [(i, (i + 1 if i % 2 else i - 1) % count) for i in range(count)]
    )
    got_last = lax.ppermute(in_pair, "dom", swaps[-2:])
    partial, kept, chosen, weights, observed = call(
        between_kernel, (pieces, first) + prepared, [SMEM] + [VMEM] * 9, 10**7, 2 * 10**6
    )(
        tile_owner, prior_velocity, sample, obs_cells[0], obs_bins[0], obs_values[0],
        in_pair, got_pair, partial, kept,
    )
    outgoing = call(
        border_kernel,
        pieces,
        [VMEM] * 8,
        10**6,
        10**6,
        scratch_shapes=[pltpu.SMEM(tile_owner.shape, jnp.int32), pltpu.SemaphoreType.DMA(())],
    )(
        tile_owner, prior_velocity, in_pair, across, got_across, got_last, kept, partial
    )
    return outgoing, chosen, weights, observed


def body(prior_sample, prior_velocity, obs_cells, obs_bins, obs_values, tile_owner):
    outgoing, chosen, weights, values = advected(
        prior_sample, prior_velocity, obs_cells, obs_bins, obs_values, tile_owner
    )
    slots, members, tile = outgoing.shape
    total = slots * members
    received = lax.all_to_all(outgoing, MEM, split_axis=0, concat_axis=0, tiled=True)
    updated = analyse(chosen, weights, values, received.reshape(total, tile))
    results = updated.reshape(slots, members, tile)
    returned = lax.all_to_all(results, MEM, split_axis=0, concat_axis=0, tiled=True)
    return restored(tile_owner, returned, prior_sample.shape)


def analyse(chosen, weights, values, ensemble):
    out = jax.ShapeDtypeStruct(ensemble.shape, BF16)
    return call(analysis_kernel, out, [VMEM] * 4, 10**9, 2 * 10**6)(chosen, weights, values, ensemble)


def restored(tile_owner, returned, shape):
    return call(
        restore_kernel,
        jax.ShapeDtypeStruct(shape, BF16),
        [SMEM, VMEM],
        10**6,
        10**6,
        out_specs=pl.BlockSpec(memory_space=pl.ANY),
        scratch_shapes=[pltpu.VMEM(shape, BF16), pltpu.SemaphoreType.DMA((shape[1],))],
    )(tile_owner, returned)


def solution(mesh):
    split = Mesh(
        mesh.devices.reshape(8, 4, 2, mesh.shape["dom"]), ("mem_0", "mem_1", "mem_2", "dom")
    )
    in_specs = (
        P(MEM, None, "dom", None),
        P(),
        P("dom", MEM, None),
        P("dom", MEM, None),
        P("dom", MEM, None),
        P("dom", None),
    )
    out_specs = P(MEM, None, "dom", None)
    return jax.shard_map(body, mesh=split, in_specs=in_specs, out_specs=out_specs, check_vma=False)
```

```python
import jax
import jax.numpy as jnp
from jax import lax
from jax.experimental import pallas as pl
from jax.experimental.pallas import tpu as pltpu
from jax.sharding import Mesh
from jax.sharding import PartitionSpec as P

STEPS = 5
MEM = ("mem_0", "mem_1", "mem_2")

advect_coef = 0.15
diffuse_coef = 0.15
loc_step = 0.35
inflation = 1.1

F32 = jnp.float32
BF16 = jnp.bfloat16
VMEM = pl.BlockSpec(memory_space=pltpu.VMEM)
SMEM = pl.BlockSpec(memory_space=pltpu.SMEM)
PARAMS = pltpu.CompilerParams(vmem_limit_bytes=48 * 1024 * 1024)


def rows_first(block):
    return jnp.swapaxes(block.astype(F32), 0, 1)


def step(rows, along_x, along_y):
    width = rows[0].shape[-1]
    below, above, inner = [], [], []
    last = len(rows) - 1
    for r, v in enumerate(rows):
        half = 0.5 * v
        flux_y = (along_y + half) * v
        below.append(v - flux_y if r >= 2 else None)
        above.append(v + flux_y if r <= last - 2 else None)
        if 1 <= r <= last - 1:
            flux_x = (along_x + half) * v
            east = pltpu.roll(v - flux_x, width - 1, axis=1)
            west = pltpu.roll(v + flux_x, 1, axis=1)
            inner.append((east + west) - 4.0 * v)
        else:
            inner.append(None)
    return [
        rows[r] + advect_coef * (inner[r] + (below[r + 1] + above[r - 1]))
        for r in range(1, last)
    ]


def edges_kernel(x_ref, out_ref, in_pair_ref, across_ref):
    out_ref[...] = x_ref[...]
    levels, rows = x_ref.shape[1], x_ref.shape[2]
    even = lax.rem(lax.axis_index("dom"), 2) == 0

    def send(low_ref, high_ref):
        for level in range(levels):
            block = x_ref[:, level]
            low_ref[level] = rows_first(block[:, 0:2]).astype(BF16)
            high_ref[level] = rows_first(block[:, rows - 2 : rows]).astype(BF16)

    @pl.when(even)
    def _():
        send(across_ref, in_pair_ref)

    @pl.when(jnp.logical_not(even))
    def _():
        send(in_pair_ref, across_ref)


def put(out_ref, slot, rows, width):
    out_ref[slot, :, 0:width] = rows[0].astype(BF16)
    out_ref[slot, :, width : 2 * width] = rows[1].astype(BF16)


def interior(slot_of, velocity_ref, x_ref, out_ref, first_ref):
    members, levels, rows, width = x_ref.shape
    pairs = rows // 2

    def one(level, carry):
        along_x = velocity_ref[0, pl.ds(level, 1), :]
        along_y = velocity_ref[1, pl.ds(level, 1), :]
        field = rows_first(x_ref[:, level])
        first = step([field[r] for r in range(rows)], along_x, along_y)
        for k, r in enumerate((0, 1, rows - 4, rows - 3)):
            first_ref[level, k] = first[r]
        done = step(first, along_x, along_y)
        for p in range(1, pairs - 1):
            put(out_ref, slot_of(level * pairs + p), done[2 * p - 2 : 2 * p], width)
        return carry

    lax.fori_loop(0, levels, one, 0, unroll=2)


def is_last():
    return lax.axis_index("dom") == lax.axis_size("dom") - 1


def in_last_pair():
    return lax.axis_index("dom") >= lax.axis_size("dom") - 2


def is_even():
    return lax.rem(lax.axis_index("dom"), 2) == 0


def interior_kernel(velocity_ref, x_ref, out_ref, first_ref):
    @pl.when(jnp.logical_not(is_last()))
    def _():
        interior(lambda tile: tile, velocity_ref, x_ref, out_ref, first_ref)


def border(at_top, owner_ref, velocity_ref, own_ref, got_ref, first_ref, out_ref, before_slots=None):
    levels, _, members, width = own_ref.shape
    pairs = owner_ref.shape[1] // levels
    top = jnp.broadcast_to(at_top.astype(jnp.int32), (members, width)) == 1
    kept = jnp.where(at_top, 0, 2)
    place = jnp.where(at_top, 0, pairs - 1)
    done = []
    for level in range(levels):
        along_x = velocity_ref[0, level : level + 1, :]
        along_y = velocity_ref[1, level : level + 1, :]
        own = [own_ref[level, k].astype(F32) for k in range(2)]
        got = [got_ref[level, k].astype(F32) for k in range(2)]
        rows = [jnp.where(top, g, o) for g, o in zip(got + own, own + got)]
        outer = step(rows, along_x, along_y)
        inner = [first_ref[level, kept + k] for k in range(2)]
        rows = [jnp.where(top, o, i) for o, i in zip(outer + inner, inner + outer)]
        done.append(step(rows, along_x, along_y))
    if before_slots is not None:
        before_slots()
    for level in range(levels):
        put(out_ref, owner_ref[0, level * pairs + place], done[level], width)


def between_kernel(
    owner_ref, velocity_ref, x_ref, cells_ref, bins_ref, values_ref, in_pair_ref, got_pair_ref, partial_ref, kept_ref,
    out_ref, first_ref, chosen_ref, weights_ref, observed_ref,
):
    tile, obs = chosen_ref.shape
    levels = x_ref.shape[1]
    pairs = owner_ref.shape[1] // levels

    @pl.when(is_last())
    def _():
        interior(lambda t: owner_ref[0, t], velocity_ref, x_ref, out_ref, first_ref)

    @pl.when(jnp.logical_not(is_last()))
    def _():
        for level in range(levels):
            for p in range(1, pairs - 1):
                out_ref[owner_ref[0, level * pairs + p]] = partial_ref[level * pairs + p]
        first_ref[...] = kept_ref[...]

    @pl.when(jnp.logical_not(in_last_pair()))
    def _():
        border(
            jnp.logical_not(is_even()), owner_ref, velocity_ref, in_pair_ref, got_pair_ref, first_ref, out_ref
        )

    rows = lax.broadcasted_iota(jnp.int32, (tile, obs), 0)
    chosen_ref[...] = jnp.where(rows == cells_ref[...], 1.0, 0.0).astype(BF16)
    weights_ref[...] = jnp.exp(-0.5 * (loc_step * bins_ref[...].astype(F32)) ** 2)
    observed_ref[...] = values_ref[...]


def border_kernel(
    slots_ref, velocity_ref, in_pair_ref, across_ref, got_across_ref, got_last_ref, first_ref, partial_ref, out_ref,
    owner_ref, arrived,
):
    slots = pltpu.make_async_copy(slots_ref, owner_ref, arrived)
    slots.start()
    border(
        is_even(), owner_ref, velocity_ref, across_ref, got_across_ref, first_ref, out_ref, before_slots=slots.wait
    )

    @pl.when(in_last_pair())
    def _():
        border(
            jnp.logical_not(is_even()), owner_ref, velocity_ref, in_pair_ref, got_last_ref, first_ref, out_ref
        )


def dot(a, b):
    return jnp.dot(a, b, preferred_element_type=F32)


def dot_t(a, b):
    return lax.dot_general(a, b, (((1,), (1,)), ((), ())), preferred_element_type=F32)


def split(x):
    high = x.astype(BF16)
    return high, (x - high.astype(F32)).astype(BF16)


def dot3(a, b):
    a_high, a_low = split(a)
    b_high, b_low = split(b)
    return dot(
        jnp.concatenate([a_low, a_high, a_high], axis=1),
        jnp.concatenate([b_high, b_low, b_high], axis=0),
    )


def thirds(row):
    first = row.astype(BF16).astype(F32)
    second = (row - first).astype(BF16).astype(F32)
    third = (row - first) - second
    which = lax.broadcasted_iota(jnp.int32, (16, row.shape[1]), 0)
    parts = jnp.where(which == 0, first, jnp.where(which == 1, second, jnp.where(which == 2, third, 0.0)))
    return parts.astype(BF16)


def whole(parts):
    return (parts[2:3] + parts[1:2]) + parts[0:1]


def analysis_kernel(chosen_ref, weights_ref, values_ref, x_ref, out_ref):
    members, tile = x_ref.shape
    obs = chosen_ref.shape[1]
    ensemble = x_ref[...].astype(F32)
    average = jnp.sum(ensemble, axis=0, keepdims=True) * (1.0 / members)
    spread = (ensemble - average).astype(BF16)
    chosen = chosen_ref[...]
    weights = weights_ref[...]
    exact = dot(spread, chosen)
    picked = exact.astype(BF16)
    scaled = (exact * weights).astype(BF16)
    across = exact.T.astype(BF16)
    ridge = (members - 1) / inflation
    sums = jnp.sum(jnp.abs(dot_t(scaled, picked)), axis=0, keepdims=True)
    norm_total = jnp.max(sums, axis=1, keepdims=True) + ridge
    over = 1.0 / norm_total
    gram = dot(across, spread)
    innovation = values_ref[...] - whole(dot(thirds(average), chosen))

    eye = jnp.where(
        lax.broadcasted_iota(jnp.int32, (obs, obs), 0) == lax.broadcasted_iota(jnp.int32, (obs, obs), 1), 1.0, 0.0
    )
    w_a = ridge * over
    w_c = eye
    w_small = w_a * eye + dot(across, scaled) * over
    z_a = 1.5 - 0.5 * w_a
    z_c = -0.5 * w_c
    z_small = 1.5 * eye - 0.5 * w_small
    for sweep in range(STEPS - 1):
        right = jnp.concatenate([w_small, w_c], axis=1)
        if sweep == 0:
            both = dot3(w_small, right)
        else:
            both = dot3(jnp.concatenate([w_small, z_small], axis=0), right)
            z_c = 1.5 * z_c - 0.5 * (both[obs:, obs:] + w_a * z_c)
            z_small = 1.5 * z_small - 0.5 * both[obs:, :obs]
            z_a = z_a * (1.5 - 0.5 * w_a)
        u_small = both[:obs, :obs]
        u_c = both[:obs, obs:] + w_a * w_c
        u_a = w_a * w_a
        f_small = 2.25 * eye - 1.5 * w_small + 0.25 * u_small
        f_c = 0.25 * u_c - 1.5 * w_c
        f_a = 2.25 - 1.5 * w_a + 0.25 * u_a
        both = dot3(w_small, jnp.concatenate([f_small, f_c], axis=1))
        w_c = both[:, obs:] + f_a * w_c
        w_small = both[:, :obs]
        w_a = w_a * f_a
    both = dot3(z_small, jnp.concatenate([w_small, w_c], axis=1))
    z_c = 1.5 * z_c - 0.5 * (both[:, obs:] + w_a * z_c)
    z_small = 1.5 * z_small - 0.5 * both[:, :obs]
    z_a = z_a * (1.5 - 0.5 * w_a)

    scale = jnp.sqrt((members - 1) * over)
    line = jnp.broadcast_to(weights * innovation, (16, obs))
    line = dot3(dot3(line, z_small), z_small) * over
    mixed = dot3(jnp.concatenate([z_c * (scale * over), line], axis=0), gram)
    high, low = split(mixed[:obs])
    rest = dot(jnp.concatenate([scaled, scaled], axis=1), jnp.concatenate([low, high], axis=0))
    base = average + mixed[obs : obs + 1]
    out_ref[...] = (base + ((scale * z_a) * spread.astype(F32) + rest)).astype(BF16)


def restore_kernel(owner_ref, x_ref, out_ref, held_ref, sent):
    members, levels, rows, width = held_ref.shape
    pairs = rows // 2

    def copy(level):
        return pltpu.make_async_copy(held_ref.at[:, level], out_ref.at[:, level], sent.at[level])

    for level in range(levels):
        tiles = [x_ref[owner_ref[0, level * pairs + p]].astype(F32) for p in range(pairs)]
        field = jnp.stack([t[:, k * width : (k + 1) * width] for t in tiles for k in range(2)])
        held_ref[:, level] = jnp.swapaxes(field, 0, 1).astype(BF16)
        copy(level).start()
    for level in range(levels):
        copy(level).wait()


def call(kernel, out, in_specs, flops, moved, out_specs=None, **more):
    return pl.pallas_call(
        kernel,
        out_shape=out,
        in_specs=in_specs,
        out_specs=jax.tree.map(lambda _: VMEM, out) if out_specs is None else out_specs,
        compiler_params=PARAMS,
        cost_estimate=pl.CostEstimate(flops=flops, bytes_accessed=moved, transcendentals=0),
        **more,
    )


def advected(prior_sample, prior_velocity, obs_cells, obs_bins, obs_values, tile_owner):
    members, levels, rows, width = prior_sample.shape
    slots, obs = tile_owner.shape[1], obs_cells.shape[2]
    tile = 2 * width
    shape = jax.ShapeDtypeStruct
    edge = shape((levels, 2, members, width), BF16)
    sample, in_pair, across = call(
        edges_kernel, (shape(prior_sample.shape, BF16), edge, edge), [VMEM], 10**5, 10**6
    )(prior_sample)
    count = lax.axis_size("dom")
    swaps = [(i, i ^ 1) for i in range(count)]
    got_pair = lax.ppermute(in_pair, "dom", swaps[:-2])
    pieces = shape((slots, members, tile), BF16)
    first = shape((levels, 4, members, width), F32)
    prepared = (shape((tile, obs), BF16), shape((1, obs), F32), shape((1, obs), F32))
    partial, kept = call(interior_kernel, (pieces, first), [VMEM] * 2, 10**7, 2 * 10**6)(
        prior_velocity, sample
    )
    ready, in_pair, partial = lax.optimization_barrier((across, in_pair, partial))
    got_across = lax.ppermute(
        ready, "dom", [(i, (i + 1 if i % 2 else i - 1) % count) for i in range(count)]
    )
    got_last = lax.ppermute(in_pair, "dom", swaps[-2:])
    partial, kept, chosen, weights, observed = call(
        between_kernel, (pieces, first) + prepared, [SMEM] + [VMEM] * 9, 10**7, 2 * 10**6
    )(
        tile_owner, prior_velocity, sample, obs_cells[0], obs_bins[0], obs_values[0],
        in_pair, got_pair, partial, kept,
    )
    outgoing = call(
        border_kernel,
        pieces,
        [VMEM] * 8,
        10**6,
        10**6,
        scratch_shapes=[pltpu.SMEM(tile_owner.shape, jnp.int32), pltpu.SemaphoreType.DMA(())],
        input_output_aliases={7: 0},
    )(
        tile_owner, prior_velocity, in_pair, across, got_across, got_last, kept, partial
    )
    return outgoing, chosen, weights, observed


def body(prior_sample, prior_velocity, obs_cells, obs_bins, obs_values, tile_owner):
    outgoing, chosen, weights, values = advected(
        prior_sample, prior_velocity, obs_cells, obs_bins, obs_values, tile_owner
    )
    slots, members, tile = outgoing.shape
    total = slots * members
    received = lax.all_to_all(outgoing, MEM, split_axis=0, concat_axis=0, tiled=True)
    updated = analyse(chosen, weights, values, received.reshape(total, tile))
    results = updated.reshape(slots, members, tile)
    returned = lax.all_to_all(results, MEM, split_axis=0, concat_axis=0, tiled=True)
    return restored(tile_owner, returned, prior_sample.shape)


def analyse(chosen, weights, values, ensemble):
    out = jax.ShapeDtypeStruct(ensemble.shape, BF16)
    return call(analysis_kernel, out, [VMEM] * 4, 10**9, 2 * 10**6)(chosen, weights, values, ensemble)


def restored(tile_owner, returned, shape):
    return call(
        restore_kernel,
        jax.ShapeDtypeStruct(shape, BF16),
        [SMEM, VMEM],
        10**6,
        10**6,
        out_specs=pl.BlockSpec(memory_space=pl.ANY),
        scratch_shapes=[pltpu.VMEM(shape, BF16), pltpu.SemaphoreType.DMA((shape[1],))],
    )(tile_owner, returned)


def solution(mesh):
    split = Mesh(
        mesh.devices.reshape(8, 4, 2, mesh.shape["dom"]), ("mem_0", "mem_1", "mem_2", "dom")
    )
    in_specs = (
        P(MEM, None, "dom", None),
        P(),
        P("dom", MEM, None),
        P("dom", MEM, None),
        P("dom", MEM, None),
        P("dom", None),
    )
    out_specs = P(MEM, None, "dom", None)
    return jax.shard_map(body, mesh=split, in_specs=in_specs, out_specs=out_specs, check_vma=False)
```

```python
import jax
import jax.numpy as jnp
from jax import lax
from jax.experimental import pallas as pl
from jax.experimental.pallas import tpu as pltpu
from jax.sharding import Mesh
from jax.sharding import PartitionSpec as P

STEPS = 5
MEM = ("mem_0", "mem_1", "mem_2")

advect_coef = 0.15
diffuse_coef = 0.15
loc_step = 0.35
inflation = 1.1

F32 = jnp.float32
BF16 = jnp.bfloat16
VMEM = pl.BlockSpec(memory_space=pltpu.VMEM)
SMEM = pl.BlockSpec(memory_space=pltpu.SMEM)
PARAMS = pltpu.CompilerParams(vmem_limit_bytes=48 * 1024 * 1024)


def rows_first(block):
    return jnp.swapaxes(block.astype(F32), 0, 1)


def step(rows, along_x, along_y):
    width = rows[0].shape[-1]
    below, above, inner = [], [], []
    last = len(rows) - 1
    for r, v in enumerate(rows):
        half = 0.5 * v
        flux_y = (along_y + half) * v
        below.append(v - flux_y if r >= 2 else None)
        above.append(v + flux_y if r <= last - 2 else None)
        if 1 <= r <= last - 1:
            flux_x = (along_x + half) * v
            east = pltpu.roll(v - flux_x, width - 1, axis=1)
            west = pltpu.roll(v + flux_x, 1, axis=1)
            inner.append((east + west) - 4.0 * v)
        else:
            inner.append(None)
    return [
        rows[r] + advect_coef * (inner[r] + (below[r + 1] + above[r - 1]))
        for r in range(1, last)
    ]


def edges_kernel(x_ref, out_ref, in_pair_ref, across_ref):
    out_ref[...] = x_ref[...]
    levels, rows = x_ref.shape[1], x_ref.shape[2]
    even = lax.rem(lax.axis_index("dom"), 2) == 0

    def send(low_ref, high_ref):
        for level in range(levels):
            block = x_ref[:, level]
            low_ref[level] = rows_first(block[:, 0:2]).astype(BF16)
            high_ref[level] = rows_first(block[:, rows - 2 : rows]).astype(BF16)

    @pl.when(even)
    def _():
        send(across_ref, in_pair_ref)

    @pl.when(jnp.logical_not(even))
    def _():
        send(in_pair_ref, across_ref)


def put(out_ref, slot, rows, width):
    out_ref[slot, :, 0:width] = rows[0].astype(BF16)
    out_ref[slot, :, width : 2 * width] = rows[1].astype(BF16)


def interior(slot_of, velocity_ref, x_ref, out_ref, first_ref):
    members, levels, rows, width = x_ref.shape
    pairs = rows // 2

    def one(level, carry):
        along_x = velocity_ref[0, pl.ds(level, 1), :]
        along_y = velocity_ref[1, pl.ds(level, 1), :]
        field = rows_first(x_ref[:, level])
        first = step([field[r] for r in range(rows)], along_x, along_y)
        for k, r in enumerate((0, 1, rows - 4, rows - 3)):
            first_ref[level, k] = first[r]
        done = step(first, along_x, along_y)
        for p in range(1, pairs - 1):
            put(out_ref, slot_of(level * pairs + p), done[2 * p - 2 : 2 * p], width)
        return carry

    lax.fori_loop(0, levels, one, 0, unroll=2)


def is_last():
    return lax.axis_index("dom") == lax.axis_size("dom") - 1


def in_last_pair():
    return lax.axis_index("dom") >= lax.axis_size("dom") - 2


def is_even():
    return lax.rem(lax.axis_index("dom"), 2) == 0


def interior_kernel(velocity_ref, x_ref, out_ref, first_ref):
    @pl.when(jnp.logical_not(is_last()))
    def _():
        interior(lambda tile: tile, velocity_ref, x_ref, out_ref, first_ref)


def border(at_top, owner_ref, velocity_ref, own_ref, got_ref, first_ref, out_ref, before_slots=None):
    levels, _, members, width = own_ref.shape
    pairs = owner_ref.shape[1] // levels
    top = jnp.broadcast_to(at_top.astype(jnp.int32), (members, width)) == 1
    kept = jnp.where(at_top, 0, 2)
    place = jnp.where(at_top, 0, pairs - 1)
    done = []
    for level in range(levels):
        along_x = velocity_ref[0, level : level + 1, :]
        along_y = velocity_ref[1, level : level + 1, :]
        own = [own_ref[level, k].astype(F32) for k in range(2)]
        got = [got_ref[level, k].astype(F32) for k in range(2)]
        rows = [jnp.where(top, g, o) for g, o in zip(got + own, own + got)]
        outer = step(rows, along_x, along_y)
        inner = [first_ref[level, kept + k] for k in range(2)]
        rows = [jnp.where(top, o, i) for o, i in zip(outer + inner, inner + outer)]
        done.append(step(rows, along_x, along_y))
    if before_slots is not None:
        before_slots()
    for level in range(levels):
        put(out_ref, owner_ref[0, level * pairs + place], done[level], width)


def between_kernel(
    owner_ref, velocity_ref, x_ref, cells_ref, bins_ref, values_ref, in_pair_ref, got_pair_ref, partial_ref, kept_ref,
    out_ref, first_ref, chosen_ref, weights_ref, observed_ref,
):
    tile, obs = chosen_ref.shape
    levels = x_ref.shape[1]
    pairs = owner_ref.shape[1] // levels

    @pl.when(is_last())
    def _():
        interior(lambda t: owner_ref[0, t], velocity_ref, x_ref, out_ref, first_ref)

    @pl.when(jnp.logical_not(is_last()))
    def _():
        for level in range(levels):
            for p in range(1, pairs - 1):
                out_ref[owner_ref[0, level * pairs + p]] = partial_ref[level * pairs + p]
        first_ref[...] = kept_ref[...]

    @pl.when(jnp.logical_not(in_last_pair()))
    def _():
        border(
            jnp.logical_not(is_even()), owner_ref, velocity_ref, in_pair_ref, got_pair_ref, first_ref, out_ref
        )

    rows = lax.broadcasted_iota(jnp.int32, (tile, obs), 0)
    chosen_ref[...] = jnp.where(rows == cells_ref[...], 1.0, 0.0).astype(BF16)
    weights_ref[...] = jnp.exp(-0.5 * (loc_step * bins_ref[...].astype(F32)) ** 2)
    observed_ref[...] = values_ref[...]


def border_kernel(
    slots_ref, velocity_ref, in_pair_ref, across_ref, got_across_ref, got_last_ref, first_ref, partial_ref, out_ref,
    owner_ref, arrived,
):
    slots = pltpu.make_async_copy(slots_ref, owner_ref, arrived)
    slots.start()
    border(
        is_even(), owner_ref, velocity_ref, across_ref, got_across_ref, first_ref, out_ref, before_slots=slots.wait
    )

    @pl.when(in_last_pair())
    def _():
        border(
            jnp.logical_not(is_even()), owner_ref, velocity_ref, in_pair_ref, got_last_ref, first_ref, out_ref
        )


def dot(a, b):
    return jnp.dot(a, b, preferred_element_type=F32)


def dot_t(a, b):
    return lax.dot_general(a, b, (((1,), (1,)), ((), ())), preferred_element_type=F32)


def split(x):
    high = x.astype(BF16)
    return high, (x - high.astype(F32)).astype(BF16)


def dot3(a, b):
    a_high, a_low = split(a)
    b_high, b_low = split(b)
    return dot(
        jnp.concatenate([a_low, a_high, a_high], axis=1),
        jnp.concatenate([b_high, b_low, b_high], axis=0),
    )


def thirds(row):
    first = row.astype(BF16).astype(F32)
    second = (row - first).astype(BF16).astype(F32)
    third = (row - first) - second
    which = lax.broadcasted_iota(jnp.int32, (16, row.shape[1]), 0)
    parts = jnp.where(which == 0, first, jnp.where(which == 1, second, jnp.where(which == 2, third, 0.0)))
    return parts.astype(BF16)


def whole(parts):
    return (parts[2:3] + parts[1:2]) + parts[0:1]


def analysis_kernel(chosen_ref, weights_ref, values_ref, x_ref, out_ref):
    members, tile = x_ref.shape
    obs = chosen_ref.shape[1]
    ensemble = x_ref[...].astype(F32)
    average = jnp.sum(ensemble, axis=0, keepdims=True) * (1.0 / members)
    spread = (ensemble - average).astype(BF16)
    chosen = chosen_ref[...]
    weights = weights_ref[...]
    exact = dot(spread, chosen)
    picked = exact.astype(BF16)
    scaled = (exact * weights).astype(BF16)
    across = exact.T.astype(BF16)
    ridge = (members - 1) / inflation
    half = members // 2
    sums = jnp.sum(jnp.abs(dot_t(scaled[:half], picked)), axis=0, keepdims=True) + jnp.sum(
        jnp.abs(dot_t(scaled[half:], picked)), axis=0, keepdims=True
    )
    norm_total = jnp.max(sums, axis=1, keepdims=True) + ridge
    over = 1.0 / norm_total
    gram = dot(across, spread)
    innovation = values_ref[...] - whole(dot(thirds(average), chosen))

    eye = jnp.where(
        lax.broadcasted_iota(jnp.int32, (obs, obs), 0) == lax.broadcasted_iota(jnp.int32, (obs, obs), 1), 1.0, 0.0
    )
    w_a = ridge * over
    w_c = eye
    w_small = w_a * eye + dot(across, scaled) * over
    z_a = 1.5 - 0.5 * w_a
    z_c = -0.5 * w_c
    z_small = 1.5 * eye - 0.5 * w_small
    for sweep in range(STEPS - 1):
        right = jnp.concatenate([w_small, w_c], axis=1)
        if sweep == 0:
            both = dot3(w_small, right)
        else:
            both = dot3(jnp.concatenate([w_small, z_small], axis=0), right)
            z_c = 1.5 * z_c - 0.5 * (both[obs:, obs:] + w_a * z_c)
            z_small = 1.5 * z_small - 0.5 * both[obs:, :obs]
            z_a = z_a * (1.5 - 0.5 * w_a)
        u_small = both[:obs, :obs]
        u_c = both[:obs, obs:] + w_a * w_c
        u_a = w_a * w_a
        f_small = 2.25 * eye - 1.5 * w_small + 0.25 * u_small
        f_c = 0.25 * u_c - 1.5 * w_c
        f_a = 2.25 - 1.5 * w_a + 0.25 * u_a
        both = dot3(w_small, jnp.concatenate([f_small, f_c], axis=1))
        w_c = both[:, obs:] + f_a * w_c
        w_small = both[:, :obs]
        w_a = w_a * f_a
    both = dot3(z_small, jnp.concatenate([w_small, w_c], axis=1))
    z_c = 1.5 * z_c - 0.5 * (both[:, obs:] + w_a * z_c)
    z_small = 1.5 * z_small - 0.5 * both[:, :obs]
    z_a = z_a * (1.5 - 0.5 * w_a)

    scale = jnp.sqrt((members - 1) * over)
    line = dot3(jnp.broadcast_to(weights * innovation, (16, obs)), z_small) * over
    mixed = dot3(jnp.concatenate([z_c * (scale * over), z_small], axis=0), gram)
    high, low = split(mixed[:obs])
    base = average + dot3(line, mixed[obs:])[0:1]
    rest = dot(jnp.concatenate([scaled, scaled], axis=1), jnp.concatenate([low, high], axis=0))
    out_ref[...] = (base + ((scale * z_a) * spread.astype(F32) + rest)).astype(BF16)


def restore_kernel(owner_ref, x_ref, out_ref, held_ref, sent):
    members, levels, rows, width = held_ref.shape
    pairs = rows // 2

    def copy(level):
        return pltpu.make_async_copy(held_ref.at[:, level], out_ref.at[:, level], sent.at[level])

    for level in range(levels):
        tiles = [x_ref[owner_ref[0, level * pairs + p]].astype(F32) for p in range(pairs)]
        field = jnp.stack([t[:, k * width : (k + 1) * width] for t in tiles for k in range(2)])
        held_ref[:, level] = jnp.swapaxes(field, 0, 1).astype(BF16)
        copy(level).start()
    for level in range(levels):
        copy(level).wait()


def call(kernel, out, in_specs, flops, moved, out_specs=None, **more):
    return pl.pallas_call(
        kernel,
        out_shape=out,
        in_specs=in_specs,
        out_specs=jax.tree.map(lambda _: VMEM, out) if out_specs is None else out_specs,
        compiler_params=PARAMS,
        cost_estimate=pl.CostEstimate(flops=flops, bytes_accessed=moved, transcendentals=0),
        **more,
    )


def advected(prior_sample, prior_velocity, obs_cells, obs_bins, obs_values, tile_owner):
    members, levels, rows, width = prior_sample.shape
    slots, obs = tile_owner.shape[1], obs_cells.shape[2]
    tile = 2 * width
    shape = jax.ShapeDtypeStruct
    edge = shape((levels, 2, members, width), BF16)
    sample, in_pair, across = call(
        edges_kernel, (shape(prior_sample.shape, BF16), edge, edge), [VMEM], 10**5, 10**6
    )(prior_sample)
    count = lax.axis_size("dom")
    swaps = [(i, i ^ 1) for i in range(count)]
    got_pair = lax.ppermute(in_pair, "dom", swaps[:-2])
    pieces = shape((slots, members, tile), BF16)
    first = shape((levels, 4, members, width), F32)
    prepared = (shape((tile, obs), BF16), shape((1, obs), F32), shape((1, obs), F32))
    partial, kept = call(interior_kernel, (pieces, first), [VMEM] * 2, 10**7, 2 * 10**6)(
        prior_velocity, sample
    )
    ready, in_pair, partial = lax.optimization_barrier((across, in_pair, partial))
    got_across = lax.ppermute(
        ready, "dom", [(i, (i + 1 if i % 2 else i - 1) % count) for i in range(count)]
    )
    got_last = lax.ppermute(in_pair, "dom", swaps[-2:])
    partial, kept, chosen, weights, observed = call(
        between_kernel, (pieces, first) + prepared, [SMEM] + [VMEM] * 9, 10**7, 2 * 10**6
    )(
        tile_owner, prior_velocity, sample, obs_cells[0], obs_bins[0], obs_values[0],
        in_pair, got_pair, partial, kept,
    )
    outgoing = call(
        border_kernel,
        pieces,
        [VMEM] * 8,
        10**6,
        10**6,
        scratch_shapes=[pltpu.SMEM(tile_owner.shape, jnp.int32), pltpu.SemaphoreType.DMA(())],
        input_output_aliases={7: 0},
    )(
        tile_owner, prior_velocity, in_pair, across, got_across, got_last, kept, partial
    )
    return outgoing, chosen, weights, observed


def body(prior_sample, prior_velocity, obs_cells, obs_bins, obs_values, tile_owner):
    outgoing, chosen, weights, values = advected(
        prior_sample, prior_velocity, obs_cells, obs_bins, obs_values, tile_owner
    )
    slots, members, tile = outgoing.shape
    total = slots * members
    received = lax.all_to_all(outgoing, MEM, split_axis=0, concat_axis=0, tiled=True)
    updated = analyse(chosen, weights, values, received.reshape(total, tile))
    results = updated.reshape(slots, members, tile)
    returned = lax.all_to_all(results, MEM, split_axis=0, concat_axis=0, tiled=True)
    return restored(tile_owner, returned, prior_sample.shape)


def analyse(chosen, weights, values, ensemble):
    out = jax.ShapeDtypeStruct(ensemble.shape, BF16)
    return call(analysis_kernel, out, [VMEM] * 4, 10**9, 2 * 10**6)(chosen, weights, values, ensemble)


def restored(tile_owner, returned, shape):
    return call(
        restore_kernel,
        jax.ShapeDtypeStruct(shape, BF16),
        [SMEM, VMEM],
        10**6,
        10**6,
        out_specs=pl.BlockSpec(memory_space=pl.ANY),
        scratch_shapes=[pltpu.VMEM(shape, BF16), pltpu.SemaphoreType.DMA((shape[1],))],
    )(tile_owner, returned)


def solution(mesh):
    split = Mesh(
        mesh.devices.reshape(8, 4, 2, mesh.shape["dom"]), ("mem_0", "mem_1", "mem_2", "dom")
    )
    in_specs = (
        P(MEM, None, "dom", None),
        P(),
        P("dom", MEM, None),
        P("dom", MEM, None),
        P("dom", MEM, None),
        P("dom", None),
    )
    out_specs = P(MEM, None, "dom", None)
    return jax.shard_map(body, mesh=split, in_specs=in_specs, out_specs=out_specs, check_vma=False)
```

```python
import jax
import jax.numpy as jnp
from jax import lax
from jax.experimental import pallas as pl
from jax.experimental.pallas import tpu as pltpu
from jax.sharding import Mesh
from jax.sharding import PartitionSpec as P

STEPS = 5
MEM = ("mem_0", "mem_1", "mem_2")

advect_coef = 0.15
diffuse_coef = 0.15
loc_step = 0.35
inflation = 1.1

F32 = jnp.float32
BF16 = jnp.bfloat16
VMEM = pl.BlockSpec(memory_space=pltpu.VMEM)
SMEM = pl.BlockSpec(memory_space=pltpu.SMEM)
PARAMS = pltpu.CompilerParams(vmem_limit_bytes=48 * 1024 * 1024)


def rows_first(block):
    return jnp.swapaxes(block.astype(F32), 0, 1)


def step(rows, along_x, along_y):
    width = rows[0].shape[-1]
    below, above, inner = [], [], []
    last = len(rows) - 1
    for r, v in enumerate(rows):
        half = 0.5 * v
        flux_y = (along_y + half) * v
        below.append(v - flux_y if r >= 2 else None)
        above.append(v + flux_y if r <= last - 2 else None)
        if 1 <= r <= last - 1:
            flux_x = (along_x + half) * v
            east = pltpu.roll(v - flux_x, width - 1, axis=1)
            west = pltpu.roll(v + flux_x, 1, axis=1)
            inner.append((east + west) - 4.0 * v)
        else:
            inner.append(None)
    return [
        rows[r] + advect_coef * (inner[r] + (below[r + 1] + above[r - 1]))
        for r in range(1, last)
    ]


def edges_kernel(x_ref, out_ref, in_pair_ref, across_ref):
    levels, rows = x_ref.shape[1], x_ref.shape[2]
    even = lax.rem(lax.axis_index("dom"), 2) == 0

    def send(low_ref, high_ref):
        for level in range(levels):
            block = x_ref[:, level]
            low_ref[level] = rows_first(block[:, 0:2]).astype(BF16)
            high_ref[level] = rows_first(block[:, rows - 2 : rows]).astype(BF16)

    @pl.when(even)
    def _():
        send(across_ref, in_pair_ref)

    @pl.when(jnp.logical_not(even))
    def _():
        send(in_pair_ref, across_ref)


def put(out_ref, slot, rows, width):
    out_ref[slot, :, 0:width] = rows[0].astype(BF16)
    out_ref[slot, :, width : 2 * width] = rows[1].astype(BF16)


def interior(slot_of, velocity_ref, x_ref, out_ref, first_ref):
    members, levels, rows, width = x_ref.shape
    pairs = rows // 2

    def one(level, carry):
        along_x = velocity_ref[0, pl.ds(level, 1), :]
        along_y = velocity_ref[1, pl.ds(level, 1), :]
        field = rows_first(x_ref[:, level])
        first = step([field[r] for r in range(rows)], along_x, along_y)
        for k, r in enumerate((0, 1, rows - 4, rows - 3)):
            first_ref[level, k] = first[r]
        done = step(first, along_x, along_y)
        for p in range(1, pairs - 1):
            put(out_ref, slot_of(level * pairs + p), done[2 * p - 2 : 2 * p], width)
        return carry

    lax.fori_loop(0, levels, one, 0, unroll=2)


def is_last():
    return lax.axis_index("dom") == lax.axis_size("dom") - 1


def in_last_pair():
    return lax.axis_index("dom") >= lax.axis_size("dom") - 2


def is_even():
    return lax.rem(lax.axis_index("dom"), 2) == 0


def interior_kernel(velocity_ref, x_ref, out_ref, first_ref):
    @pl.when(jnp.logical_not(is_last()))
    def _():
        interior(lambda tile: tile, velocity_ref, x_ref, out_ref, first_ref)


def border(at_top, owner_ref, velocity_ref, own_ref, got_ref, first_ref, out_ref, before_slots=None):
    levels, _, members, width = own_ref.shape
    pairs = owner_ref.shape[1] // levels
    top = jnp.broadcast_to(at_top.astype(jnp.int32), (members, width)) == 1
    kept = jnp.where(at_top, 0, 2)
    place = jnp.where(at_top, 0, pairs - 1)
    done = []
    for level in range(levels):
        along_x = velocity_ref[0, level : level + 1, :]
        along_y = velocity_ref[1, level : level + 1, :]
        own = [own_ref[level, k].astype(F32) for k in range(2)]
        got = [got_ref[level, k].astype(F32) for k in range(2)]
        rows = [jnp.where(top, g, o) for g, o in zip(got + own, own + got)]
        outer = step(rows, along_x, along_y)
        inner = [first_ref[level, kept + k] for k in range(2)]
        rows = [jnp.where(top, o, i) for o, i in zip(outer + inner, inner + outer)]
        done.append(step(rows, along_x, along_y))
    if before_slots is not None:
        before_slots()
    for level in range(levels):
        put(out_ref, owner_ref[0, level * pairs + place], done[level], width)


def between_kernel(
    owner_ref, velocity_ref, x_ref, cells_ref, bins_ref, values_ref, in_pair_ref, got_pair_ref, partial_ref, kept_ref,
    out_ref, first_ref, chosen_ref, weights_ref, observed_ref,
):
    tile, obs = chosen_ref.shape
    levels = x_ref.shape[1]
    pairs = owner_ref.shape[1] // levels

    @pl.when(is_last())
    def _():
        interior(lambda t: owner_ref[0, t], velocity_ref, x_ref, out_ref, first_ref)

    @pl.when(jnp.logical_not(is_last()))
    def _():
        for level in range(levels):
            for p in range(1, pairs - 1):
                out_ref[owner_ref[0, level * pairs + p]] = partial_ref[level * pairs + p]
        first_ref[...] = kept_ref[...]

    @pl.when(jnp.logical_not(in_last_pair()))
    def _():
        border(
            jnp.logical_not(is_even()), owner_ref, velocity_ref, in_pair_ref, got_pair_ref, first_ref, out_ref
        )

    rows = lax.broadcasted_iota(jnp.int32, (tile, obs), 0)
    chosen_ref[...] = jnp.where(rows == cells_ref[...], 1.0, 0.0).astype(BF16)
    weights_ref[...] = jnp.exp(-0.5 * (loc_step * bins_ref[...].astype(F32)) ** 2)
    observed_ref[...] = values_ref[...]


def border_kernel(
    slots_ref, velocity_ref, in_pair_ref, across_ref, got_across_ref, got_last_ref, first_ref, partial_ref, out_ref,
    owner_ref, arrived,
):
    slots = pltpu.make_async_copy(slots_ref, owner_ref, arrived)
    slots.start()
    border(
        is_even(), owner_ref, velocity_ref, across_ref, got_across_ref, first_ref, out_ref, before_slots=slots.wait
    )

    @pl.when(in_last_pair())
    def _():
        border(
            jnp.logical_not(is_even()), owner_ref, velocity_ref, in_pair_ref, got_last_ref, first_ref, out_ref
        )


def dot(a, b):
    return jnp.dot(a, b, preferred_element_type=F32)


def dot_t(a, b):
    return lax.dot_general(a, b, (((1,), (1,)), ((), ())), preferred_element_type=F32)


def split(x):
    high = x.astype(BF16)
    return high, (x - high.astype(F32)).astype(BF16)


def dot3(a, b):
    a_high, a_low = split(a)
    b_high, b_low = split(b)
    return dot(
        jnp.concatenate([a_low, a_high, a_high], axis=1),
        jnp.concatenate([b_high, b_low, b_high], axis=0),
    )


def thirds(row):
    first = row.astype(BF16).astype(F32)
    second = (row - first).astype(BF16).astype(F32)
    third = (row - first) - second
    which = lax.broadcasted_iota(jnp.int32, (16, row.shape[1]), 0)
    parts = jnp.where(which == 0, first, jnp.where(which == 1, second, jnp.where(which == 2, third, 0.0)))
    return parts.astype(BF16)


def whole(parts):
    return (parts[2:3] + parts[1:2]) + parts[0:1]


def analysis_kernel(chosen_ref, weights_ref, values_ref, x_ref, out_ref):
    members, tile = x_ref.shape
    obs = chosen_ref.shape[1]
    ensemble = x_ref[...].astype(F32)
    average = jnp.sum(ensemble, axis=0, keepdims=True) * (1.0 / members)
    spread = (ensemble - average).astype(BF16)
    chosen = chosen_ref[...]
    weights = weights_ref[...]
    exact = dot(spread, chosen)
    picked = exact.astype(BF16)
    scaled = (exact * weights).astype(BF16)
    across = exact.T.astype(BF16)
    ridge = (members - 1) / inflation
    half = members // 2
    sums = jnp.sum(jnp.abs(dot_t(scaled[:half], picked)), axis=0, keepdims=True) + jnp.sum(
        jnp.abs(dot_t(scaled[half:], picked)), axis=0, keepdims=True
    )
    norm_total = jnp.max(sums, axis=1, keepdims=True) + ridge
    over = 1.0 / norm_total
    gram = dot(across, spread)
    innovation = values_ref[...] - whole(dot(thirds(average), chosen))

    eye = jnp.where(
        lax.broadcasted_iota(jnp.int32, (obs, obs), 0) == lax.broadcasted_iota(jnp.int32, (obs, obs), 1), 1.0, 0.0
    )
    w_a = ridge * over
    w_c = eye
    w_small = w_a * eye + dot(across, scaled) * over
    z_a = 1.5 - 0.5 * w_a
    z_c = -0.5 * w_c
    z_small = 1.5 * eye - 0.5 * w_small
    for sweep in range(STEPS - 1):
        right = jnp.concatenate([w_small, w_c], axis=1)
        if sweep == 0:
            both = dot3(w_small, right)
        else:
            both = dot3(jnp.concatenate([w_small, z_small], axis=0), right)
            z_c = 1.5 * z_c - 0.5 * (both[obs:, obs:] + w_a * z_c)
            z_small = 1.5 * z_small - 0.5 * both[obs:, :obs]
            z_a = z_a * (1.5 - 0.5 * w_a)
        u_small = both[:obs, :obs]
        u_c = both[:obs, obs:] + w_a * w_c
        u_a = w_a * w_a
        f_small = 2.25 * eye - 1.5 * w_small + 0.25 * u_small
        f_c = 0.25 * u_c - 1.5 * w_c
        f_a = 2.25 - 1.5 * w_a + 0.25 * u_a
        both = dot3(w_small, jnp.concatenate([f_small, f_c], axis=1))
        w_c = both[:, obs:] + f_a * w_c
        w_small = both[:, :obs]
        w_a = w_a * f_a
    both = dot3(z_small, jnp.concatenate([w_small, w_c], axis=1))
    z_c = 1.5 * z_c - 0.5 * (both[:, obs:] + w_a * z_c)
    z_small = 1.5 * z_small - 0.5 * both[:, :obs]
    z_a = z_a * (1.5 - 0.5 * w_a)

    scale = jnp.sqrt((members - 1) * over)
    line = dot3(jnp.broadcast_to(weights * innovation, (16, obs)), z_small) * over
    mixed = dot3(jnp.concatenate([z_c * (scale * over), z_small], axis=0), gram)
    high, low = split(mixed[:obs])
    base = average + dot3(line, mixed[obs:])[0:1]
    rest = dot(jnp.concatenate([scaled, scaled], axis=1), jnp.concatenate([low, high], axis=0))
    out_ref[...] = (base + ((scale * z_a) * spread.astype(F32) + rest)).astype(BF16)


def restore_kernel(owner_ref, x_ref, out_ref, held_ref, sent):
    members, levels, rows, width = held_ref.shape
    pairs = rows // 2

    def copy(level):
        return pltpu.make_async_copy(held_ref.at[:, level], out_ref.at[:, level], sent.at[level])

    for level in range(levels):
        tiles = [x_ref[owner_ref[0, level * pairs + p]].astype(F32) for p in range(pairs)]
        field = jnp.stack([t[:, k * width : (k + 1) * width] for t in tiles for k in range(2)])
        held_ref[:, level] = jnp.swapaxes(field, 0, 1).astype(BF16)
        copy(level).start()
    for level in range(levels):
        copy(level).wait()


def call(kernel, out, in_specs, flops, moved, out_specs=None, **more):
    return pl.pallas_call(
        kernel,
        out_shape=out,
        in_specs=in_specs,
        out_specs=jax.tree.map(lambda _: VMEM, out) if out_specs is None else out_specs,
        compiler_params=PARAMS,
        cost_estimate=pl.CostEstimate(flops=flops, bytes_accessed=moved, transcendentals=0),
        **more,
    )


def advected(prior_sample, prior_velocity, obs_cells, obs_bins, obs_values, tile_owner):
    members, levels, rows, width = prior_sample.shape
    slots, obs = tile_owner.shape[1], obs_cells.shape[2]
    tile = 2 * width
    shape = jax.ShapeDtypeStruct
    edge = shape((levels, 2, members, width), BF16)
    sample, in_pair, across = call(
        edges_kernel,
        (shape(prior_sample.shape, BF16), edge, edge),
        [VMEM],
        10**5,
        10**6,
        input_output_aliases={0: 0},
    )(prior_sample)
    count = lax.axis_size("dom")
    swaps = [(i, i ^ 1) for i in range(count)]
    got_pair = lax.ppermute(in_pair, "dom", swaps[:-2])
    pieces = shape((slots, members, tile), BF16)
    first = shape((levels, 4, members, width), F32)
    prepared = (shape((tile, obs), BF16), shape((1, obs), F32), shape((1, obs), F32))
    partial, kept = call(interior_kernel, (pieces, first), [VMEM] * 2, 10**7, 2 * 10**6)(
        prior_velocity, sample
    )
    ready, in_pair, partial = lax.optimization_barrier((across, in_pair, partial))
    got_across = lax.ppermute(
        ready, "dom", [(i, (i + 1 if i % 2 else i - 1) % count) for i in range(count)]
    )
    got_last = lax.ppermute(in_pair, "dom", swaps[-2:])
    partial, kept, chosen, weights, observed = call(
        between_kernel, (pieces, first) + prepared, [SMEM] + [VMEM] * 9, 10**7, 2 * 10**6
    )(
        tile_owner, prior_velocity, sample, obs_cells[0], obs_bins[0], obs_values[0],
        in_pair, got_pair, partial, kept,
    )
    outgoing = call(
        border_kernel,
        pieces,
        [VMEM] * 8,
        10**6,
        10**6,
        scratch_shapes=[pltpu.SMEM(tile_owner.shape, jnp.int32), pltpu.SemaphoreType.DMA(())],
        input_output_aliases={7: 0},
    )(
        tile_owner, prior_velocity, in_pair, across, got_across, got_last, kept, partial
    )
    return outgoing, chosen, weights, observed


def body(prior_sample, prior_velocity, obs_cells, obs_bins, obs_values, tile_owner):
    outgoing, chosen, weights, values = advected(
        prior_sample, prior_velocity, obs_cells, obs_bins, obs_values, tile_owner
    )
    slots, members, tile = outgoing.shape
    total = slots * members
    received = lax.all_to_all(outgoing, MEM, split_axis=0, concat_axis=0, tiled=True)
    updated = analyse(chosen, weights, values, received.reshape(total, tile))
    results = updated.reshape(slots, members, tile)
    returned = lax.all_to_all(results, MEM, split_axis=0, concat_axis=0, tiled=True)
    return restored(tile_owner, returned, prior_sample.shape)


def analyse(chosen, weights, values, ensemble):
    out = jax.ShapeDtypeStruct(ensemble.shape, BF16)
    return call(analysis_kernel, out, [VMEM] * 4, 10**9, 2 * 10**6)(chosen, weights, values, ensemble)


def restored(tile_owner, returned, shape):
    return call(
        restore_kernel,
        jax.ShapeDtypeStruct(shape, BF16),
        [SMEM, VMEM],
        10**6,
        10**6,
        out_specs=pl.BlockSpec(memory_space=pl.ANY),
        scratch_shapes=[pltpu.VMEM(shape, BF16), pltpu.SemaphoreType.DMA((shape[1],))],
    )(tile_owner, returned)


def solution(mesh):
    split = Mesh(
        mesh.devices.reshape(8, 4, 2, mesh.shape["dom"]), ("mem_0", "mem_1", "mem_2", "dom")
    )
    in_specs = (
        P(MEM, None, "dom", None),
        P(),
        P("dom", MEM, None),
        P("dom", MEM, None),
        P("dom", MEM, None),
        P("dom", None),
    )
    out_specs = P(MEM, None, "dom", None)
    return jax.shard_map(body, mesh=split, in_specs=in_specs, out_specs=out_specs, check_vma=False)
```

```python
import jax
import jax.numpy as jnp
from jax import lax
from jax.experimental import pallas as pl
from jax.experimental.pallas import tpu as pltpu
from jax.sharding import Mesh
from jax.sharding import PartitionSpec as P

STEPS = 5
MEM = ("mem_0", "mem_1", "mem_2")
SENT = ("mem_1", "mem_2", "mem_0")

advect_coef = 0.15
diffuse_coef = 0.15
loc_step = 0.35
inflation = 1.1

F32 = jnp.float32
BF16 = jnp.bfloat16
VMEM = pl.BlockSpec(memory_space=pltpu.VMEM)
SMEM = pl.BlockSpec(memory_space=pltpu.SMEM)
PARAMS = pltpu.CompilerParams(vmem_limit_bytes=48 * 1024 * 1024)


def rows_first(block):
    return jnp.swapaxes(block.astype(F32), 0, 1)


def step(rows, along_x, along_y):
    width = rows[0].shape[-1]
    below, above, inner = [], [], []
    last = len(rows) - 1
    for r, v in enumerate(rows):
        half = 0.5 * v
        flux_y = (along_y + half) * v
        below.append(v - flux_y if r >= 2 else None)
        above.append(v + flux_y if r <= last - 2 else None)
        if 1 <= r <= last - 1:
            flux_x = (along_x + half) * v
            east = pltpu.roll(v - flux_x, width - 1, axis=1)
            west = pltpu.roll(v + flux_x, 1, axis=1)
            inner.append((east + west) - 4.0 * v)
        else:
            inner.append(None)
    return [
        rows[r] + advect_coef * (inner[r] + (below[r + 1] + above[r - 1]))
        for r in range(1, last)
    ]


def edges_kernel(x_ref, out_ref, in_pair_ref, across_ref):
    out_ref[...] = x_ref[...]
    levels, rows = x_ref.shape[1], x_ref.shape[2]
    even = lax.rem(lax.axis_index("dom"), 2) == 0

    def send(low_ref, high_ref):
        for level in range(levels):
            block = x_ref[:, level]
            low_ref[level] = rows_first(block[:, 0:2]).astype(BF16)
            high_ref[level] = rows_first(block[:, rows - 2 : rows]).astype(BF16)

    @pl.when(even)
    def _():
        send(across_ref, in_pair_ref)

    @pl.when(jnp.logical_not(even))
    def _():
        send(in_pair_ref, across_ref)


def put(out_ref, slot, rows, width):
    out_ref[slot, :, 0:width] = rows[0].astype(BF16)
    out_ref[slot, :, width : 2 * width] = rows[1].astype(BF16)


def interior(slot_of, velocity_ref, x_ref, out_ref, first_ref):
    members, levels, rows, width = x_ref.shape
    pairs = rows // 2

    def one(level, carry):
        along_x = velocity_ref[0, pl.ds(level, 1), :]
        along_y = velocity_ref[1, pl.ds(level, 1), :]
        field = rows_first(x_ref[:, level])
        first = step([field[r] for r in range(rows)], along_x, along_y)
        for k, r in enumerate((0, 1, rows - 4, rows - 3)):
            first_ref[level, k] = first[r]
        done = step(first, along_x, along_y)
        for p in range(1, pairs - 1):
            put(out_ref, slot_of(level * pairs + p), done[2 * p - 2 : 2 * p], width)
        return carry

    lax.fori_loop(0, levels, one, 0, unroll=2)


def place_of(owner_ref, tile):
    slots, first = owner_ref.shape[1], lax.axis_size("mem_0")
    slot = owner_ref[0, tile]
    return lax.rem(slot, slots // first) * first + lax.div(slot, slots // first)


def is_last():
    return lax.axis_index("dom") == lax.axis_size("dom") - 1


def in_last_pair():
    return lax.axis_index("dom") >= lax.axis_size("dom") - 2


def is_even():
    return lax.rem(lax.axis_index("dom"), 2) == 0


def interior_kernel(velocity_ref, x_ref, out_ref, first_ref):
    @pl.when(jnp.logical_not(is_last()))
    def _():
        interior(lambda tile: tile, velocity_ref, x_ref, out_ref, first_ref)


def border(at_top, owner_ref, velocity_ref, own_ref, got_ref, first_ref, out_ref, before_slots=None):
    levels, _, members, width = own_ref.shape
    pairs = owner_ref.shape[1] // levels
    top = jnp.broadcast_to(at_top.astype(jnp.int32), (members, width)) == 1
    kept = jnp.where(at_top, 0, 2)
    place = jnp.where(at_top, 0, pairs - 1)
    done = []
    for level in range(levels):
        along_x = velocity_ref[0, level : level + 1, :]
        along_y = velocity_ref[1, level : level + 1, :]
        own = [own_ref[level, k].astype(F32) for k in range(2)]
        got = [got_ref[level, k].astype(F32) for k in range(2)]
        rows = [jnp.where(top, g, o) for g, o in zip(got + own, own + got)]
        outer = step(rows, along_x, along_y)
        inner = [first_ref[level, kept + k] for k in range(2)]
        rows = [jnp.where(top, o, i) for o, i in zip(outer + inner, inner + outer)]
        done.append(step(rows, along_x, along_y))
    if before_slots is not None:
        before_slots()
    for level in range(levels):
        put(out_ref, place_of(owner_ref, level * pairs + place), done[level], width)


def between_kernel(
    owner_ref, velocity_ref, x_ref, cells_ref, bins_ref, values_ref, in_pair_ref, got_pair_ref, partial_ref, kept_ref,
    out_ref, first_ref, chosen_ref, weights_ref, observed_ref,
):
    tile, obs = chosen_ref.shape
    levels = x_ref.shape[1]
    pairs = owner_ref.shape[1] // levels

    @pl.when(is_last())
    def _():
        interior(lambda t: place_of(owner_ref, t), velocity_ref, x_ref, out_ref, first_ref)

    @pl.when(jnp.logical_not(is_last()))
    def _():
        for level in range(levels):
            for p in range(1, pairs - 1):
                out_ref[place_of(owner_ref, level * pairs + p)] = partial_ref[level * pairs + p]
        first_ref[...] = kept_ref[...]

    @pl.when(jnp.logical_not(in_last_pair()))
    def _():
        border(
            jnp.logical_not(is_even()), owner_ref, velocity_ref, in_pair_ref, got_pair_ref, first_ref, out_ref
        )

    rows = lax.broadcasted_iota(jnp.int32, (tile, obs), 0)
    chosen_ref[...] = jnp.where(rows == cells_ref[...], 1.0, 0.0).astype(BF16)
    weights_ref[...] = jnp.exp(-0.5 * (loc_step * bins_ref[...].astype(F32)) ** 2)
    observed_ref[...] = values_ref[...]


def border_kernel(
    slots_ref, velocity_ref, in_pair_ref, across_ref, got_across_ref, got_last_ref, first_ref, partial_ref, out_ref,
    owner_ref, arrived,
):
    slots = pltpu.make_async_copy(slots_ref, owner_ref, arrived)
    slots.start()
    border(
        is_even(), owner_ref, velocity_ref, across_ref, got_across_ref, first_ref, out_ref, before_slots=slots.wait
    )

    @pl.when(in_last_pair())
    def _():
        border(
            jnp.logical_not(is_even()), owner_ref, velocity_ref, in_pair_ref, got_last_ref, first_ref, out_ref
        )


def dot(a, b):
    return jnp.dot(a, b, preferred_element_type=F32)


def dot_t(a, b):
    return lax.dot_general(a, b, (((1,), (1,)), ((), ())), preferred_element_type=F32)


def split(x):
    high = x.astype(BF16)
    return high, (x - high.astype(F32)).astype(BF16)


def dot3(a, b):
    a_high, a_low = split(a)
    b_high, b_low = split(b)
    return dot(
        jnp.concatenate([a_low, a_high, a_high], axis=1),
        jnp.concatenate([b_high, b_low, b_high], axis=0),
    )


def thirds(row):
    first = row.astype(BF16).astype(F32)
    second = (row - first).astype(BF16).astype(F32)
    third = (row - first) - second
    which = lax.broadcasted_iota(jnp.int32, (16, row.shape[1]), 0)
    parts = jnp.where(which == 0, first, jnp.where(which == 1, second, jnp.where(which == 2, third, 0.0)))
    return parts.astype(BF16)


def whole(parts):
    return (parts[2:3] + parts[1:2]) + parts[0:1]


def analysis_kernel(chosen_ref, weights_ref, values_ref, x_ref, out_ref):
    members, tile = x_ref.shape
    obs = chosen_ref.shape[1]
    ensemble = x_ref[...].astype(F32)
    average = jnp.sum(ensemble, axis=0, keepdims=True) * (1.0 / members)
    spread = (ensemble - average).astype(BF16)
    chosen = chosen_ref[...]
    weights = weights_ref[...]
    exact = dot(spread, chosen)
    picked = exact.astype(BF16)
    scaled = (exact * weights).astype(BF16)
    across = exact.T.astype(BF16)
    ridge = (members - 1) / inflation
    half = members // 2
    sums = jnp.sum(jnp.abs(dot_t(scaled[:half], picked)), axis=0, keepdims=True) + jnp.sum(
        jnp.abs(dot_t(scaled[half:], picked)), axis=0, keepdims=True
    )
    norm_total = jnp.max(sums, axis=1, keepdims=True) + ridge
    over = 1.0 / norm_total
    gram = dot(across, spread)
    innovation = values_ref[...] - whole(dot(thirds(average), chosen))

    eye = jnp.where(
        lax.broadcasted_iota(jnp.int32, (obs, obs), 0) == lax.broadcasted_iota(jnp.int32, (obs, obs), 1), 1.0, 0.0
    )
    w_a = ridge * over
    w_c = eye
    w_small = w_a * eye + dot(across, scaled) * over
    z_a = 1.5 - 0.5 * w_a
    z_c = -0.5 * w_c
    z_small = 1.5 * eye - 0.5 * w_small
    for sweep in range(STEPS - 1):
        right = jnp.concatenate([w_small, w_c], axis=1)
        if sweep == 0:
            both = dot3(w_small, right)
        else:
            both = dot3(jnp.concatenate([w_small, z_small], axis=0), right)
            z_c = 1.5 * z_c - 0.5 * (both[obs:, obs:] + w_a * z_c)
            z_small = 1.5 * z_small - 0.5 * both[obs:, :obs]
            z_a = z_a * (1.5 - 0.5 * w_a)
        u_small = both[:obs, :obs]
        u_c = both[:obs, obs:] + w_a * w_c
        u_a = w_a * w_a
        f_small = 2.25 * eye - 1.5 * w_small + 0.25 * u_small
        f_c = 0.25 * u_c - 1.5 * w_c
        f_a = 2.25 - 1.5 * w_a + 0.25 * u_a
        both = dot3(w_small, jnp.concatenate([f_small, f_c], axis=1))
        w_c = both[:, obs:] + f_a * w_c
        w_small = both[:, :obs]
        w_a = w_a * f_a
    both = dot3(z_small, jnp.concatenate([w_small, w_c], axis=1))
    z_c = 1.5 * z_c - 0.5 * (both[:, obs:] + w_a * z_c)
    z_small = 1.5 * z_small - 0.5 * both[:, :obs]
    z_a = z_a * (1.5 - 0.5 * w_a)

    scale = jnp.sqrt((members - 1) * over)
    line = dot3(jnp.broadcast_to(weights * innovation, (16, obs)), z_small) * over
    mixed = dot3(jnp.concatenate([z_c * (scale * over), z_small], axis=0), gram)
    high, low = split(mixed[:obs])
    base = average + dot3(line, mixed[obs:])[0:1]
    rest = dot(jnp.concatenate([scaled, scaled], axis=1), jnp.concatenate([low, high], axis=0))
    out_ref[...] = (base + ((scale * z_a) * spread.astype(F32) + rest)).astype(BF16)


def restore_kernel(owner_ref, x_ref, out_ref, held_ref, sent):
    members, levels, rows, width = held_ref.shape
    pairs = rows // 2

    def copy(level):
        return pltpu.make_async_copy(held_ref.at[:, level], out_ref.at[:, level], sent.at[level])

    for level in range(levels):
        tiles = [x_ref[place_of(owner_ref, level * pairs + p)].astype(F32) for p in range(pairs)]
        field = jnp.stack([t[:, k * width : (k + 1) * width] for t in tiles for k in range(2)])
        held_ref[:, level] = jnp.swapaxes(field, 0, 1).astype(BF16)
        copy(level).start()
    for level in range(levels):
        copy(level).wait()


def call(kernel, out, in_specs, flops, moved, out_specs=None, **more):
    return pl.pallas_call(
        kernel,
        out_shape=out,
        in_specs=in_specs,
        out_specs=jax.tree.map(lambda _: VMEM, out) if out_specs is None else out_specs,
        compiler_params=PARAMS,
        cost_estimate=pl.CostEstimate(flops=flops, bytes_accessed=moved, transcendentals=0),
        **more,
    )


def advected(prior_sample, prior_velocity, obs_cells, obs_bins, obs_values, tile_owner):
    members, levels, rows, width = prior_sample.shape
    slots, obs = tile_owner.shape[1], obs_cells.shape[2]
    tile = 2 * width
    shape = jax.ShapeDtypeStruct
    edge = shape((levels, 2, members, width), BF16)
    sample, in_pair, across = call(
        edges_kernel, (shape(prior_sample.shape, BF16), edge, edge), [VMEM], 10**5, 10**6
    )(prior_sample)
    count = lax.axis_size("dom")
    swaps = [(i, i ^ 1) for i in range(count)]
    got_pair = lax.ppermute(in_pair, "dom", swaps[:-2])
    pieces = shape((slots, members, tile), BF16)
    first = shape((levels, 4, members, width), F32)
    prepared = (shape((tile, obs), BF16), shape((1, obs), F32), shape((1, obs), F32))
    partial, kept = call(interior_kernel, (pieces, first), [VMEM] * 2, 10**7, 2 * 10**6)(
        prior_velocity, sample
    )
    ready, in_pair, partial = lax.optimization_barrier((across, in_pair, partial))
    got_across = lax.ppermute(
        ready, "dom", [(i, (i + 1 if i % 2 else i - 1) % count) for i in range(count)]
    )
    got_last = lax.ppermute(in_pair, "dom", swaps[-2:])
    partial, kept, chosen, weights, observed = call(
        between_kernel, (pieces, first) + prepared, [SMEM] + [VMEM] * 9, 10**7, 2 * 10**6
    )(
        tile_owner, prior_velocity, sample, obs_cells[0], obs_bins[0], obs_values[0],
        in_pair, got_pair, partial, kept,
    )
    outgoing = call(
        border_kernel,
        pieces,
        [VMEM] * 8,
        10**6,
        10**6,
        scratch_shapes=[pltpu.SMEM(tile_owner.shape, jnp.int32), pltpu.SemaphoreType.DMA(())],
        input_output_aliases={7: 0},
    )(
        tile_owner, prior_velocity, in_pair, across, got_across, got_last, kept, partial
    )
    return outgoing, chosen, weights, observed


def body(prior_sample, prior_velocity, obs_cells, obs_bins, obs_values, tile_owner):
    outgoing, chosen, weights, values = advected(
        prior_sample, prior_velocity, obs_cells, obs_bins, obs_values, tile_owner
    )
    slots, members, tile = outgoing.shape
    total = slots * members
    received = lax.all_to_all(outgoing, SENT, split_axis=0, concat_axis=0, tiled=True)
    updated = analyse(chosen, weights, values, received.reshape(total, tile))
    results = updated.reshape(slots, members, tile)
    returned = lax.all_to_all(results, SENT, split_axis=0, concat_axis=0, tiled=True)
    return restored(tile_owner, returned, prior_sample.shape)


def analyse(chosen, weights, values, ensemble):
    out = jax.ShapeDtypeStruct(ensemble.shape, BF16)
    return call(analysis_kernel, out, [VMEM] * 4, 10**9, 2 * 10**6)(chosen, weights, values, ensemble)


def restored(tile_owner, returned, shape):
    return call(
        restore_kernel,
        jax.ShapeDtypeStruct(shape, BF16),
        [SMEM, VMEM],
        10**6,
        10**6,
        out_specs=pl.BlockSpec(memory_space=pl.ANY),
        scratch_shapes=[pltpu.VMEM(shape, BF16), pltpu.SemaphoreType.DMA((shape[1],))],
    )(tile_owner, returned)


def solution(mesh):
    split = Mesh(
        mesh.devices.reshape(8, 4, 2, mesh.shape["dom"]), ("mem_0", "mem_1", "mem_2", "dom")
    )
    in_specs = (
        P(MEM, None, "dom", None),
        P(),
        P("dom", MEM, None),
        P("dom", MEM, None),
        P("dom", MEM, None),
        P("dom", None),
    )
    out_specs = P(MEM, None, "dom", None)
    return jax.shard_map(body, mesh=split, in_specs=in_specs, out_specs=out_specs, check_vma=False)
```
